512 devices in a mesh: grp: 2 (over z_lo), seq: 64 (over x, y, core), mdl: 4 (over z_hi).
Axes of the slice: x: 4, y: 8, z: 8 (z_hi: 4, z_lo: 2; z = z_hi * 2 + z_lo), core: 2. Of those that a mesh axis runs over, the one named last changes fastest.
Arguments:
- audio: bfloat16 [49152, 1280], P('seq'), may hold values from -6 to 6
- frame_count: int32 [1], replicated, may hold values from 24576 to 49152
- ln_gain: float32 [1280], replicated, may hold values from 0.1 to 1.9
- glu_weight: bfloat16 [2, 1280, 1280], P(None, None, 'mdl'), may hold values from -0.15625 to 0.15625
- dw_kernel: float32 [31, 1280], P(None, 'mdl'), may hold values from -1 to 1
- pw_weight: bfloat16 [1280, 1280], P('mdl'), may hold values from -0.15625 to 0.15625
- adapt_weight: bfloat16 [1280, 3584], P('seq', 'mdl'), may hold values from -0.15625 to 0.15625
- text: bfloat16 [12288, 3584], P('seq', 'mdl'), may hold values from -6 to 6
- norm_gain: float32 [3584], replicated, may hold values from 0.1 to 1.9
- qkv_weight: bfloat16 [3584, 4608], P('seq', 'mdl'), may hold values from -0.09375 to 0.09375
- qkv_bias: float32 [4608], P('mdl'), may hold values from -3 to 3
Outputs:
- sectioned: bfloat16 [2, 12288, 3584], P('grp', 'seq', 'mdl')
The draws below stay inside these ranges and needn't reach their ends.
All inputs are finite; a program needn't handle non-finite values.
Results may differ from the reference program's by a relative error of at most 0.02.
Values may be sent and summed in bfloat16 or wider, within the bound.
No kernel may reach another device: no remote copies, remote signals or barrier semaphores. Data moves between devices by JAX's collectives and lax.ppermute only.
A program may use at most 64 MiB of HBM per device.

```python
import jax
import jax.numpy as jnp
from jax import lax

E = 1280
KERNEL = 31
D = 3584
HEADS = 28
KV = 4
HEAD = 128
A = 192
FRAMES = 49152
QKV = 4608
N_SEQ = 64
N_MDL = 4


def level_of(key, dims, split, least, high):
    loudness = 1.0
    for position, parts in split:
        draws = jax.random.uniform(jax.random.fold_in(jax.random.fold_in(key, 6), position), (parts,), jnp.float32, least / len(split), high / len(split))
        loudness = loudness * jnp.repeat(jnp.exp(draws), dims[position] // parts).reshape((-1,) + (1,) * (len(dims) - 1 - position))
    return loudness


def normal_values(own_key, dims, deviation, bound, split=(), held_as=jnp.bfloat16):
    values = jax.random.normal(own_key, dims, jnp.float32) * deviation
    if len(split) > 0:
        values = level_of(own_key, dims, split, -0.22, 0.18) * values
    return jnp.clip(values, min=-bound, max=bound).astype(held_as)


def setup_inputs(seed: int = 0) -> dict:
    arg_keys = jax.random.split(jax.random.key(seed), 12)
    return {
        "audio": normal_values(arg_keys[0], (FRAMES, E), 1.0, 6.0, ((0, 64),)),
        "frame_count": jax.random.randint(arg_keys[1], (1,), FRAMES // 2, FRAMES + 1).astype(jnp.int32),
        "ln_gain": jnp.clip(1.0 + 0.18 * jax.random.normal(arg_keys[2], (E,), jnp.float32), 0.1, 1.9),
        "glu_weight": normal_values(arg_keys[3], (2, E, E), E ** -0.5, 0.15625, ((2, 4),)),
        "dw_kernel": normal_values(arg_keys[4], (KERNEL, E), KERNEL ** -0.5, 1.0, ((1, 4),), jnp.float32),
        "pw_weight": normal_values(arg_keys[5], (E, E), E ** -0.5, 0.15625, ((0, 4),)),
        "adapt_weight": normal_values(arg_keys[6], (E, D), E ** -0.5, 0.15625, ((0, 64), (1, 4))),
        "text": normal_values(arg_keys[7], (N_SEQ * A, D), 1.0, 6.0, ((0, 64), (1, 4))),
        "norm_gain": jnp.clip(1.0 + 0.18 * jax.random.normal(arg_keys[8], (D,), jnp.float32), 0.1, 1.9),
        "qkv_weight": normal_values(arg_keys[9], (D, QKV), D ** -0.5, 0.09375, ((0, 64), (1, 4))),
        "qkv_bias": normal_values(arg_keys[10], (QKV,), 0.5, 3.0, ((0, 4),), jnp.float32),
    }


def rotate(values, positions):
    half = values.shape[-1] // 2
    freq = 1000000.0 ** (-(jnp.arange(half, dtype=jnp.float32) * 2.0 / values.shape[-1]))
    angle = positions.astype(jnp.float32)[:, None] * freq[None, :]
    cosine = jnp.cos(angle)[:, None, :]
    sine = jnp.sin(angle)[:, None, :]
    first = values[..., :half]
    second = values[..., half:]
    return jnp.concatenate([first * cosine - second * sine, second * cosine + first * sine], axis=-1)

def reference(audio, frame_count, ln_gain, glu_weight, dw_kernel, pw_weight, adapt_weight, text, norm_gain, qkv_weight, qkv_bias):
    rows = audio.astype(jnp.float32)
    centred = rows - lax.optimization_barrier(jnp.mean(rows, axis=-1, keepdims=True))
    spread = lax.optimization_barrier(jnp.mean(centred * centred, axis=-1, keepdims=True))
    normed = (centred * lax.rsqrt(spread + 1e-05) * ln_gain).astype(jnp.bfloat16)
    valid = (jnp.arange(FRAMES, dtype=jnp.int32) < frame_count[0]).astype(jnp.float32)
    left = jnp.dot(normed, glu_weight[0], preferred_element_type=jnp.float32)
    right = jnp.dot(normed, glu_weight[1], preferred_element_type=jnp.float32)
    gated = (left * jax.nn.sigmoid(right) * valid[:, None]).astype(jnp.bfloat16)
    margin = (KERNEL - 1) // 2
    padded = jnp.pad(gated, ((margin, margin), (0, 0))).astype(jnp.float32)
    conv = jnp.zeros((FRAMES, E), jnp.float32)
    for offset in range(KERNEL):
        conv = conv + padded[offset:offset + FRAMES] * dw_kernel[offset]
    act = (conv * jax.nn.sigmoid(conv)).astype(jnp.bfloat16)
    block = E // N_MDL
    total = lax.optimization_barrier(jnp.mean(rows.reshape(FRAMES // 4, 4, E), axis=1))
    for index in range(N_MDL):
        term = jnp.dot(act[:, index * block:(index + 1) * block], pw_weight[index * block:(index + 1) * block], preferred_element_type=jnp.float32)
        term = lax.optimization_barrier(jnp.mean(term.reshape(FRAMES // 4, 4, E), axis=1)).astype(jnp.bfloat16)
        term = lax.optimization_barrier(term)
        total = total + term.astype(jnp.float32)
    pooled = total.astype(jnp.bfloat16)
    tokens = jnp.dot(pooled, adapt_weight, preferred_element_type=jnp.float32).astype(jnp.bfloat16)
    per_block = QKV // N_MDL
    query_cols = HEADS // N_MDL * HEAD
    key_cols = KV // N_MDL * HEAD
    shaped = qkv_weight.reshape(D, N_MDL, per_block)
    w_query = shaped[:, :, :query_cols].reshape(D, HEADS * HEAD)
    w_key = shaped[:, :, query_cols:query_cols + key_cols].reshape(D, KV * HEAD)
    w_value = shaped[:, :, query_cols + key_cols:].reshape(D, KV * HEAD)
    bias_shaped = qkv_bias.reshape(N_MDL, per_block)
    b_query = bias_shaped[:, :query_cols].reshape(HEADS * HEAD)
    b_key = bias_shaped[:, query_cols:query_cols + key_cols].reshape(KV * HEAD)
    b_value = bias_shaped[:, query_cols + key_cols:].reshape(KV * HEAD)
    group = HEADS // KV
    positions = jnp.arange(2 * A, dtype=jnp.int32)
    allowed = (positions[None, :] <= positions[A:][:, None]).astype(jnp.float32)

    def one_sequence(pair):
        sound, words = pair
        joined = jnp.concatenate([sound, words], axis=0).astype(jnp.float32)
        scale_rows = lax.rsqrt(lax.optimization_barrier(jnp.mean(joined * joined, axis=-1, keepdims=True)) + 1e-06)
        normal_rows = (joined * scale_rows * norm_gain).astype(jnp.bfloat16)
        query = jnp.dot(normal_rows, w_query, preferred_element_type=jnp.float32) + b_query
        keys = jnp.dot(normal_rows, w_key, preferred_element_type=jnp.float32) + b_key
        values = jnp.dot(normal_rows, w_value, preferred_element_type=jnp.float32) + b_value
        query = rotate(query.reshape(2 * A, HEADS, HEAD), positions).astype(jnp.bfloat16)
        keys = rotate(keys.reshape(2 * A, KV, HEAD), positions).astype(jnp.bfloat16)
        values = values.reshape(2 * A, KV, HEAD).astype(jnp.bfloat16)
        asked = query[A:].reshape(A, KV, group, HEAD).astype(jnp.float32)
        scores = jnp.einsum('qkgd,pkd->kgqp', asked, keys.astype(jnp.float32)) / jnp.sqrt(jnp.float32(HEAD))
        weights = jnp.exp(scores) * allowed
        probs = (weights / lax.optimization_barrier(jnp.sum(weights, axis=-1, keepdims=True))).astype(jnp.bfloat16)
        context = jnp.einsum('kgqp,pkd->qkgd', probs.astype(jnp.float32), values.astype(jnp.float32))
        return context.reshape(A, HEADS * HEAD).astype(jnp.bfloat16)
    contexts = lax.map(one_sequence, (tokens.reshape(N_SEQ, A, D), text.reshape(N_SEQ, A, D)))
    return jnp.stack([tokens, contexts.reshape(N_SEQ * A, D)])
```

```python
import functools

import jax
import jax.numpy as jnp
from jax import lax
from jax.experimental import pallas as pl
from jax.experimental.pallas import tpu as pltpu
from jax.sharding import PartitionSpec as P

HEADS = 28
KV = 4
HEAD = 128
VMEM = 48 * 1024 * 1024


def rotary_tables(count):
    half = HEAD // 2
    freq = 1000000.0 ** (-(jnp.arange(half, dtype=jnp.float32) * 2.0 / HEAD))
    angle = jnp.arange(count, dtype=jnp.int32).astype(jnp.float32)[:, None] * freq[None, :]
    cosine, sine = jnp.cos(angle), jnp.sin(angle)
    return jnp.concatenate([cosine, cosine], 1), jnp.concatenate([-sine, sine], 1)


def turned(values, cosine, sine):
    return values * cosine + pltpu.roll(values, HEAD // 2, 1) * sine


def text_kernel(x_ref, gain_ref, w_ref, bias_ref, cos_ref, sin_ref, q_ref, k_ref, v_ref, acc, square):
    step = pl.program_id(0)

    @pl.when(step == 0)
    def _():
        acc[...] = jnp.zeros_like(acc)
        square[...] = jnp.zeros_like(square)

    x = x_ref[0].astype(jnp.float32)
    square[...] += jnp.sum(x * x, axis=1, keepdims=True)
    acc[...] += jnp.dot(
        (x * gain_ref[0]).astype(jnp.bfloat16), w_ref[...], preferred_element_type=jnp.float32
    )

    @pl.when(step == pl.num_programs(0) - 1)
    def _():
        scale = lax.rsqrt(square[...] / (pl.num_programs(0) * x.shape[1]) + 1e-6)
        cosine, sine = cos_ref[...], sin_ref[...]
        heads = q_ref.shape[1] // HEAD
        for h in range(heads + 2):
            cols = pl.ds(h * HEAD, HEAD)
            value = acc[:, cols] * scale + bias_ref[:, cols]
            if h < heads + 1:
                value = turned(value, cosine, sine)
            value = value.astype(jnp.bfloat16)
            if h < heads:
                q_ref[:, cols] = value
            elif h == heads:
                k_ref[...] = value
            else:
                v_ref[...] = value


def audio_kernel(
    order_ref, *refs, parts
):
    xs = refs[:parts]
    (gain_ref, wk_ref, wv_ref, bias_ref, cos_ref, sin_ref, q_ref, kt_ref, vt_ref, out_ref, acc_k, acc_v, square) = refs[parts:]
    step = pl.program_id(0)

    @pl.when(step == 0)
    def _():
        acc_k[...] = jnp.zeros_like(acc_k)
        acc_v[...] = jnp.zeros_like(acc_v)
        square[...] = jnp.zeros_like(square)

    for i in range(parts):

        @pl.when(step == i)
        def _():
            x = xs[i][...].astype(jnp.float32)
            square[...] += jnp.sum(x * x, axis=1, keepdims=True)
            xg = (x * gain_ref[0]).astype(jnp.bfloat16)
            acc_k[...] += jnp.dot(xg, wk_ref[...], preferred_element_type=jnp.float32)
            acc_v[...] += jnp.dot(xg, wv_ref[...], preferred_element_type=jnp.float32)

    @pl.when(step == pl.num_programs(0) - 1)
    def _():
        count = acc_k.shape[0]
        heads = q_ref.shape[1] // HEAD
        scale = lax.rsqrt(square[...] / (parts * xs[0].shape[1]) + 1e-6)
        keys = turned(acc_k[...] * scale + bias_ref[:, :HEAD], cos_ref[...], sin_ref[...])
        keys = jnp.concatenate([keys.astype(jnp.bfloat16), kt_ref[...]], axis=0)
        values = (acc_v[...] * scale + bias_ref[:, HEAD:]).astype(jnp.bfloat16)
        values = jnp.concatenate([values, vt_ref[...]], axis=0)
        row = lax.broadcasted_iota(jnp.int32, (count, 2 * count), 0)
        col = lax.broadcasted_iota(jnp.int32, (count, 2 * count), 1)
        allowed = col <= row + count
        for h in range(heads):
            cols = pl.ds(h * HEAD, HEAD)
            scores = lax.dot_general(
                q_ref[:, cols], keys, (((1,), (1,)), ((), ())), preferred_element_type=jnp.float32
            ) * (HEAD**-0.5)
            scores = jnp.where(allowed, scores, -1e30)
            weights = jnp.exp(scores - jnp.max(scores, axis=1, keepdims=True))
            probs = weights * (1.0 / jnp.sum(weights, axis=1, keepdims=True))
            out_ref[:, cols] = jnp.dot(
                probs.astype(jnp.bfloat16), values, preferred_element_type=jnp.float32
            ).astype(jnp.bfloat16)


def text_part(x, gain, weight, bias, tables):
    parts, count, width = x.shape
    total = weight.shape[1]
    heads = total // HEAD - 2
    cosine, sine = tables
    whole = lambda *shape: pl.BlockSpec(shape, lambda k: (0,) * len(shape))
    return pl.pallas_call(
        text_kernel,
        grid=(parts,),
        in_specs=[
            pl.BlockSpec((1, count, width), lambda k: (k, 0, 0)),
            pl.BlockSpec((1, 1, width), lambda k: (k, 0, 0)),
            pl.BlockSpec((width, total), lambda k: (k, 0)),
            whole(1, total),
            pl.BlockSpec((count, HEAD), lambda k: (1, 0)),
            pl.BlockSpec((count, HEAD), lambda k: (1, 0)),
        ],
        out_specs=[whole(count, heads * HEAD), whole(count, HEAD), whole(count, HEAD)],
        out_shape=[
            jax.ShapeDtypeStruct((count, heads * HEAD), jnp.bfloat16),
            jax.ShapeDtypeStruct((count, HEAD), jnp.bfloat16),
            jax.ShapeDtypeStruct((count, HEAD), jnp.bfloat16),
        ],
        scratch_shapes=[pltpu.VMEM((count, total), jnp.float32), pltpu.VMEM((count, 1), jnp.float32)],
        compiler_params=pltpu.CompilerParams(vmem_limit_bytes=VMEM),
        cost_estimate=pl.CostEstimate(
            flops=2 * count * parts * width * total, bytes_accessed=2 * parts * width * (total + count), transcendentals=0
        ),
        name="text_part",
    )(x, gain, weight, bias, cosine, sine)


def audio_part(order, xs, gain, weight, bias, tables, q, kt, vt):
    parts = len(xs)
    count, width = xs[0].shape
    total = weight.shape[1]
    heads = total // HEAD - 2
    cosine, sine = tables
    whole = lambda *shape: pl.BlockSpec(shape, lambda k, o: (0,) * len(shape))
    return pl.pallas_call(
        functools.partial(audio_kernel, parts=parts),
        grid_spec=pltpu.PrefetchScalarGridSpec(
            num_scalar_prefetch=1,
            grid=(parts,),
            in_specs=[whole(count, width)] * parts
            + [
                pl.BlockSpec((1, 1, width), lambda k, o: (o[k], 0, 0)),
                pl.BlockSpec((width, HEAD), lambda k, o: (o[k], heads)),
                pl.BlockSpec((width, HEAD), lambda k, o: (o[k], heads + 1)),
                whole(1, 2 * HEAD),
                whole(count, HEAD),
                whole(count, HEAD),
                whole(count, heads * HEAD),
                whole(count, HEAD),
                whole(count, HEAD),
            ],
            out_specs=whole(count, heads * HEAD),
            scratch_shapes=[
                pltpu.VMEM((count, HEAD), jnp.float32),
                pltpu.VMEM((count, HEAD), jnp.float32),
                pltpu.VMEM((count, 1), jnp.float32),
            ],
        ),
        out_shape=jax.ShapeDtypeStruct((count, heads * HEAD), jnp.bfloat16),
        compiler_params=pltpu.CompilerParams(vmem_limit_bytes=VMEM),
        cost_estimate=pl.CostEstimate(
            flops=2 * count * parts * width * 2 * HEAD, bytes_accessed=2 * parts * width * (2 * HEAD + count), transcendentals=0
        ),
        name="audio_part",
    )(order, *xs, gain, weight, weight, bias, cosine[:count], sine[:count], q, kt, vt)


def pooling(rows):
    r = lax.broadcasted_iota(jnp.int32, (rows // 4, rows), 0)
    c = lax.broadcasted_iota(jnp.int32, (rows // 4, rows), 1)
    return jnp.where(c // 4 == r, 0.25, 0.0).astype(jnp.bfloat16)


def encode(audio, frame_count, ln_gain, glu_weight, dw_kernel, pw_weight):
    frames_dev = audio.shape[0]
    rows = audio.astype(jnp.float32)
    centred = rows - jnp.mean(rows, axis=-1, keepdims=True)
    spread = jnp.mean(centred * centred, axis=-1, keepdims=True)
    normed = (centred * lax.rsqrt(spread + 1e-05) * ln_gain).astype(jnp.bfloat16)
    first_frame = lax.axis_index("seq") * frames_dev
    valid = (first_frame + jnp.arange(frames_dev, dtype=jnp.int32) < frame_count[0]).astype(
        jnp.float32
    )
    left = jnp.dot(normed, glu_weight[0], preferred_element_type=jnp.float32)
    right = jnp.dot(normed, glu_weight[1], preferred_element_type=jnp.float32)
    gated = (left * jax.nn.sigmoid(right) * valid[:, None]).astype(jnp.bfloat16)
    taps = dw_kernel.shape[0]
    margin = (taps - 1) // 2
    count = lax.axis_size("seq")
    up = [(i, i + 1) for i in range(count - 1)]
    down = [(j, i) for i, j in up]
    before = lax.ppermute(gated[frames_dev - margin :], "seq", up)
    after = lax.ppermute(gated[:margin], "seq", down)
    padded = jnp.concatenate([before, gated, after], axis=0)
    conv = jnp.zeros(gated.shape, jnp.float32)
    for offset in range(taps):
        conv = conv + padded[offset : offset + frames_dev].astype(jnp.float32) * dw_kernel[offset]
    act = (conv * jax.nn.sigmoid(conv)).astype(jnp.bfloat16)
    pool = pooling(frames_dev)
    pooled_act = jnp.dot(pool, act, preferred_element_type=jnp.float32).astype(jnp.bfloat16)
    term = jnp.dot(pooled_act, pw_weight, preferred_element_type=jnp.float32).astype(jnp.bfloat16)
    pooled_audio = jnp.dot(pool, audio, preferred_element_type=jnp.float32)
    return term, pooled_audio


def gather_rows(block):
    return lax.all_gather(block, "seq", axis=0, tiled=True)


def shards(
    audio, frame_count, ln_gain, glu_weight, dw_kernel, pw_weight, adapt_weight, text, norm_gain, qkv_weight, qkv_bias
):
    grp = lax.axis_index("grp")
    mdl = lax.axis_index("mdl")
    n_mdl = lax.axis_size("mdl")
    both = ("grp", "mdl")
    width = adapt_weight.shape[1]
    held = jnp.pad(
        adapt_weight,
        ((0, qkv_weight.shape[0] - adapt_weight.shape[0]), (0, qkv_weight.shape[1] - width)),
    )
    gathered = gather_rows(jnp.where(grp == 0, held, qkv_weight))

    words = [text] + [
        lax.ppermute(text, both, [(n_mdl + i, n_mdl + (i + k) % n_mdl) for i in range(n_mdl)])
        for k in range(1, n_mdl)
    ]
    term, pooled_audio = encode(audio, frame_count, ln_gain, glu_weight, dw_kernel, pw_weight)
    total = pooled_audio + term.astype(jnp.float32)
    for k in range(1, n_mdl):
        total = total + lax.ppermute(
            term, both, [(i, (i + k) % n_mdl) for i in range(n_mdl)]
        ).astype(jnp.float32)
    pooled = total.astype(jnp.bfloat16)
    n_seq = lax.axis_size("seq")
    adapter = gathered.reshape(n_seq, qkv_weight.shape[0], -1)[:, : adapt_weight.shape[0], :width]
    adapter = adapter.reshape(n_seq * adapt_weight.shape[0], width)
    tokens = jnp.dot(pooled, adapter, preferred_element_type=jnp.float32).astype(jnp.bfloat16)

    tables = rotary_tables(2 * text.shape[0])
    gain = norm_gain.reshape(n_mdl, 1, width)
    order = (mdl - jnp.arange(n_mdl, dtype=jnp.int32)) % n_mdl
    x = jnp.stack(words)
    x = jnp.stack([lax.dynamic_index_in_dim(x, (mdl - i) % n_mdl, 0, keepdims=False) for i in range(n_mdl)])
    q, kt, vt = text_part(x, gain, gathered, qkv_bias[None], tables)
    sounds = [
        lax.ppermute(tokens, both, [(i, n_mdl + (i + k) % n_mdl) for i in range(n_mdl)])
        for k in range(n_mdl)
    ]
    context = audio_part(order, sounds, gain, gathered, qkv_bias[None, -2 * HEAD :], tables, q, kt, vt)
    return jnp.where(grp == 0, tokens, context)[None]


def solution(mesh):
    in_specs = (
        P("seq", None),
        P(),
        P(),
        P(None, None, "mdl"),
        P(None, "mdl"),
        P("mdl", None),
        P("seq", "mdl"),
        P("seq", "mdl"),
        P(),
        P("seq", "mdl"),
        P("mdl"),
    )
    out_specs = P("grp", "seq", "mdl")
    return jax.shard_map(shards, mesh=mesh, in_specs=in_specs, out_specs=out_specs, check_vma=False)
```

```python
import functools

import jax
import jax.numpy as jnp
from jax import lax
from jax.experimental import pallas as pl
from jax.experimental.pallas import tpu as pltpu
from jax.sharding import PartitionSpec as P

HEADS = 28
KV = 4
HEAD = 128
VMEM = 48 * 1024 * 1024
NX = 4
NY = 8
ADAPT_SLOT = 48
ADAPT_COLS = 896


def rotary_tables(count):
    half = HEAD // 2
    freq = 1000000.0 ** (-(jnp.arange(half, dtype=jnp.float32) * 2.0 / HEAD))
    angle = jnp.arange(count, dtype=jnp.int32).astype(jnp.float32)[:, None] * freq[None, :]
    cosine, sine = jnp.cos(angle), jnp.sin(angle)
    return jnp.concatenate([cosine, cosine], 1), jnp.concatenate([-sine, sine], 1)


def turned(values, cosine, sine):
    return values * cosine + pltpu.roll(values, HEAD // 2, 1) * sine


def text_kernel(order_ref, *refs, parts):
    xs = refs[:parts]
    gain_ref, w_ref, bias_ref, cos_ref, sin_ref, q_ref, k_ref, v_ref, acc, square = refs[parts:]
    step = pl.program_id(0)

    @pl.when(step == 0)
    def _():
        acc[...] = jnp.zeros_like(acc)
        square[...] = jnp.zeros_like(square)

    for i in range(parts):

        @pl.when(step == i)
        def _():
            x = xs[i][...].astype(jnp.float32)
            square[...] += jnp.sum(x * x, axis=1, keepdims=True)
            acc[...] += jnp.dot(
                (x * gain_ref[0]).astype(jnp.bfloat16), w_ref[...], preferred_element_type=jnp.float32
            )

    @pl.when(step == pl.num_programs(0) - 1)
    def _():
        scale = lax.rsqrt(square[...] / (parts * xs[0].shape[1]) + 1e-6)
        cosine, sine = cos_ref[...], sin_ref[...]
        heads = q_ref.shape[1] // HEAD
        for h in range(heads + 2):
            cols = pl.ds(h * HEAD, HEAD)
            value = acc[:, cols] * scale + bias_ref[:, cols]
            if h < heads + 1:
                value = turned(value, cosine, sine)
            value = value.astype(jnp.bfloat16)
            if h < heads:
                q_ref[:, cols] = value
            elif h == heads:
                k_ref[...] = value
            else:
                v_ref[...] = value


def audio_kernel(
    order_ref, *refs, parts
):
    xs = refs[:parts]
    (gain_ref, wk_ref, wv_ref, bias_ref, cos_ref, sin_ref, q_ref, kt_ref, vt_ref, out_ref, acc_k, acc_v, square) = refs[parts:]
    step = pl.program_id(0)

    @pl.when(step == 0)
    def _():
        acc_k[...] = jnp.zeros_like(acc_k)
        acc_v[...] = jnp.zeros_like(acc_v)
        square[...] = jnp.zeros_like(square)

    for i in range(parts):

        @pl.when(step == i)
        def _():
            x = xs[i][...].astype(jnp.float32)
            square[...] += jnp.sum(x * x, axis=1, keepdims=True)
            xg = (x * gain_ref[0]).astype(jnp.bfloat16)
            acc_k[...] += jnp.dot(xg, wk_ref[...], preferred_element_type=jnp.float32)
            acc_v[...] += jnp.dot(xg, wv_ref[...], preferred_element_type=jnp.float32)

    @pl.when(step == pl.num_programs(0) - 1)
    def _():
        count = acc_k.shape[0]
        heads = q_ref.shape[1] // HEAD
        scale = lax.rsqrt(square[...] / (parts * xs[0].shape[1]) + 1e-6)
        keys = turned(acc_k[...] * scale + bias_ref[:, :HEAD], cos_ref[...], sin_ref[...])
        keys = jnp.concatenate([keys.astype(jnp.bfloat16), kt_ref[...]], axis=0)
        values = (acc_v[...] * scale + bias_ref[:, HEAD:]).astype(jnp.bfloat16)
        values = jnp.concatenate([values, vt_ref[...]], axis=0)
        row = lax.broadcasted_iota(jnp.int32, (count, 2 * count), 0)
        col = lax.broadcasted_iota(jnp.int32, (count, 2 * count), 1)
        allowed = col <= row + count
        for h in range(heads):
            cols = pl.ds(h * HEAD, HEAD)
            scores = lax.dot_general(
                q_ref[:, cols], keys, (((1,), (1,)), ((), ())), preferred_element_type=jnp.float32
            ) * (HEAD**-0.5)
            scores = jnp.where(allowed, scores, -1e30)
            weights = jnp.exp(scores - jnp.max(scores, axis=1, keepdims=True))
            probs = weights * (1.0 / jnp.sum(weights, axis=1, keepdims=True))
            out_ref[:, cols] = jnp.dot(
                probs.astype(jnp.bfloat16), values, preferred_element_type=jnp.float32
            ).astype(jnp.bfloat16)


def text_part(order, xs, gain, weight, bias, tables):
    parts = len(xs)
    count, width = xs[0].shape
    total = weight.shape[1]
    heads = total // HEAD - 2
    cosine, sine = tables
    whole = lambda *shape: pl.BlockSpec(shape, lambda k, o: (0,) * len(shape))
    return pl.pallas_call(
        functools.partial(text_kernel, parts=parts),
        grid_spec=pltpu.PrefetchScalarGridSpec(
            num_scalar_prefetch=1,
            grid=(parts,),
            in_specs=[whole(count, width)] * parts
            + [
                pl.BlockSpec((1, 1, width), lambda k, o: (o[k], 0, 0)),
                pl.BlockSpec((width, total), lambda k, o: (o[k], 0)),
                whole(1, total),
                whole(count, HEAD),
                whole(count, HEAD),
            ],
            out_specs=[whole(count, heads * HEAD), whole(count, HEAD), whole(count, HEAD)],
            scratch_shapes=[pltpu.VMEM((count, total), jnp.float32), pltpu.VMEM((count, 1), jnp.float32)],
        ),
        out_shape=[
            jax.ShapeDtypeStruct((count, heads * HEAD), jnp.bfloat16),
            jax.ShapeDtypeStruct((count, HEAD), jnp.bfloat16),
            jax.ShapeDtypeStruct((count, HEAD), jnp.bfloat16),
        ],
        compiler_params=pltpu.CompilerParams(vmem_limit_bytes=VMEM),
        cost_estimate=pl.CostEstimate(
            flops=2 * count * parts * width * total, bytes_accessed=2 * parts * width * (total + count), transcendentals=0
        ),
        name="text_part",
    )(order, *xs, gain, weight, bias, cosine[count:], sine[count:])


def audio_part(order, xs, gain, weight, bias, tables, q, kt, vt):
    parts = len(xs)
    count, width = xs[0].shape
    total = weight.shape[1]
    heads = total // HEAD - 2
    cosine, sine = tables
    whole = lambda *shape: pl.BlockSpec(shape, lambda k, o: (0,) * len(shape))
    return pl.pallas_call(
        functools.partial(audio_kernel, parts=parts),
        grid_spec=pltpu.PrefetchScalarGridSpec(
            num_scalar_prefetch=1,
            grid=(parts,),
            in_specs=[whole(count, width)] * parts
            + [
                pl.BlockSpec((1, 1, width), lambda k, o: (o[k], 0, 0)),
                pl.BlockSpec((width, HEAD), lambda k, o: (o[k], heads)),
                pl.BlockSpec((width, HEAD), lambda k, o: (o[k], heads + 1)),
                whole(1, 2 * HEAD),
                whole(count, HEAD),
                whole(count, HEAD),
                whole(count, heads * HEAD),
                whole(count, HEAD),
                whole(count, HEAD),
            ],
            out_specs=whole(count, heads * HEAD),
            scratch_shapes=[
                pltpu.VMEM((count, HEAD), jnp.float32),
                pltpu.VMEM((count, HEAD), jnp.float32),
                pltpu.VMEM((count, 1), jnp.float32),
            ],
        ),
        out_shape=jax.ShapeDtypeStruct((count, heads * HEAD), jnp.bfloat16),
        compiler_params=pltpu.CompilerParams(vmem_limit_bytes=VMEM),
        cost_estimate=pl.CostEstimate(
            flops=2 * count * parts * width * 2 * HEAD, bytes_accessed=2 * parts * width * (2 * HEAD + count), transcendentals=0
        ),
        name="audio_part",
    )(order, *xs, gain, weight, weight, bias, cosine[:count], sine[:count], q, kt, vt)


def pooling(rows):
    r = lax.broadcasted_iota(jnp.int32, (rows // 4, rows), 0)
    c = lax.broadcasted_iota(jnp.int32, (rows // 4, rows), 1)
    return jnp.where((c >= 4 * r) & (c < 4 * r + 4), 0.25, 0.0).astype(jnp.bfloat16)


def dot_t(a, b):
    return lax.dot_general(a, b, (((1,), (1,)), ((), ())), preferred_element_type=jnp.float32)


def gate_kernel(count_ref, audio_ref, gain_ref, weight_ref, gated_ref, pooled_ref):
    audio = audio_ref[...]
    rows = audio.astype(jnp.float32)
    centred = rows - jnp.mean(rows, axis=1, keepdims=True)
    spread = jnp.mean(centred * centred, axis=1, keepdims=True)
    normed = (centred * lax.rsqrt(spread + 1e-5) * gain_ref[...]).astype(jnp.bfloat16)
    left = dot_t(normed, weight_ref[0])
    right = dot_t(normed, weight_ref[1])
    frame = pl.program_id(0) * rows.shape[0] + lax.broadcasted_iota(jnp.int32, (rows.shape[0], 1), 0)
    gated = left * (1.0 / (1.0 + jnp.exp(-right)))
    gated_ref[...] = jnp.where(frame < count_ref[0], gated, 0.0).astype(gated_ref.dtype)
    pooled_ref[...] = jnp.dot(pooling(rows.shape[0]), audio, preferred_element_type=jnp.float32)


def gate(left_frames, audio, gain, weight):
    frames, width = audio.shape
    columns = weight.shape[1]
    block = 256
    return pl.pallas_call(
        gate_kernel,
        grid=(frames // block,),
        in_specs=[
            pl.BlockSpec(memory_space=pltpu.SMEM),
            pl.BlockSpec((block, width), lambda i: (i, 0)),
            pl.BlockSpec((1, width), lambda i: (0, 0)),
            pl.BlockSpec((2, columns, width), lambda i: (0, 0, 0)),
        ],
        out_specs=[
            pl.BlockSpec((block, columns), lambda i: (i, 0)),
            pl.BlockSpec((block // 4, width), lambda i: (i, 0)),
        ],
        out_shape=[
            jax.ShapeDtypeStruct((frames, columns), jnp.bfloat16),
            jax.ShapeDtypeStruct((frames // 4, width), jnp.float32),
        ],
        compiler_params=pltpu.CompilerParams(vmem_limit_bytes=VMEM),
        cost_estimate=pl.CostEstimate(
            flops=4 * frames * width * columns, bytes_accessed=2 * frames * width * 4, transcendentals=frames * columns
        ),
        name="gate",
    )(left_frames, audio, gain, weight)


EDGE = 16


def conv_kernel(before_ref, gated_ref, after_ref, taps_ref, pw_ref, *refs):
    term_ref, padded, act = refs[-3:]
    frames, columns = gated_ref.shape
    taps = taps_ref.shape[0]
    padded[:EDGE] = before_ref[...].astype(jnp.float32)
    padded[EDGE : EDGE + frames] = gated_ref[...].astype(jnp.float32)
    padded[EDGE + frames :] = after_ref[...].astype(jnp.float32)
    chunk = 64
    lead = EDGE - (taps - 1) // 2
    for at in range(0, columns, 128):
        lanes = slice(at, min(at + 128, columns))

        def body(i, carry, lanes=lanes):
            first = pl.multiple_of(i * chunk, chunk)
            window = padded[pl.ds(first, chunk + 2 * EDGE), lanes]
            total = jnp.zeros((chunk, window.shape[1]), jnp.float32)
            for turn in range(8):
                turned_by = window if turn == 0 else pltpu.roll(window, window.shape[0] - turn, 0)
                for offset in range(turn, lead + taps, 8):
                    if offset >= lead:
                        start = offset - turn
                        total = total + turned_by[start : start + chunk] * taps_ref[offset - lead, lanes][None]
            value = total * (1.0 / (1.0 + jnp.exp(-total)))
            act[pl.ds(first, chunk), lanes] = value.astype(jnp.bfloat16)
            return carry

        lax.fori_loop(0, frames // chunk, body, 0)
    pooled = jnp.dot(pooling(frames), act[...], preferred_element_type=jnp.float32).astype(jnp.bfloat16)
    term_ref[...] = jnp.dot(pooled, pw_ref[...], preferred_element_type=jnp.float32).astype(term_ref.dtype)


def conv(before, gated, after, taps, pw, *after_these):
    frames, columns = gated.shape
    vmem = pl.BlockSpec(memory_space=pltpu.VMEM)
    return pl.pallas_call(
        conv_kernel,
        in_specs=[vmem] * 5 + [pl.BlockSpec(memory_space=pl.ANY)] * len(after_these),
        out_specs=vmem,
        out_shape=jax.ShapeDtypeStruct((frames // 4, pw.shape[1]), jnp.bfloat16),
        scratch_shapes=[
            pltpu.VMEM((frames + 2 * EDGE, columns), jnp.float32),
            pltpu.VMEM((frames, columns), jnp.bfloat16),
        ],
        compiler_params=pltpu.CompilerParams(vmem_limit_bytes=VMEM),
        cost_estimate=pl.CostEstimate(
            flops=5_000_000_000, bytes_accessed=2 * frames * columns * 4, transcendentals=frames * columns
        ),
        name="conv",
    )(before, gated, after, taps, pw, *after_these)


def place(shift_x, shift_y):
    return [
        ((x * NY + y) * 2 + c, ((x + shift_x) % NX * NY + (y + shift_y) % NY) * 2 + c)
        for x in range(NX)
        for y in range(NY)
        for c in range(2)
    ]


SWAP = [(i, i ^ 1) for i in range(NX * NY * 2)]


def of_group(group, pairs):
    count = NX * NY * 2
    return [(group * count + i, group * count + j) for i, j in pairs]


def spread(block):
    send = lambda v, dx, dy: lax.ppermute(v, "seq", place(dx, dy))
    near = jnp.concatenate([send(block, 0, 1), block, send(block, 0, -1)], axis=0)
    before = send(near, -1, 0)
    behind = send(near, 1, 0)
    far = jnp.concatenate([send(near, 0, 3), send(near[:2], 0, -3)], axis=0)
    inner, outer = [-1, 0, 1], [-4, -3, -2, 2, 3]
    before_far = send(far, -1, 0)
    behind_far = send(far, 1, 0)
    second = send(before, -1, 0)
    groups = ("grp", "seq")
    second_far = lax.ppermute(behind_far, groups, of_group(1, place(1, 0)))
    direct = lax.ppermute(far[:, :ADAPT_SLOT, :ADAPT_COLS], groups, of_group(0, place(2, 0)))
    pieces = [
        (0, inner, near),
        (0, outer, far),
        (-1, inner, behind),
        (1, inner, before),
        (-1, outer, behind_far),
        (1, outer, before_far),
        (2, inner, second),
        (2, outer, second_far),
    ]
    return pieces, direct


def join_kernel(index_ref, *refs, counts):
    ins, out, sem = refs[: len(counts)], refs[len(counts)], refs[len(counts) + 1]
    copies = []
    at = 0
    for ref, count in zip(ins, counts, strict=True):
        for j in range(count):
            copy = pltpu.make_async_copy(ref.at[j], out.at[index_ref[at]], sem.at[at])
            copy.start()
            copies.append(copy)
            at += 1
    for copy in copies:
        copy.wait()


def join(index, pieces):
    counts = [p.shape[0] for p in pieces]
    rows, columns = pieces[0].shape[1:]
    total = sum(counts)
    return pl.pallas_call(
        functools.partial(join_kernel, counts=counts),
        in_specs=[pl.BlockSpec(memory_space=pltpu.SMEM)] + [pl.BlockSpec(memory_space=pl.ANY)] * len(pieces),
        out_specs=pl.BlockSpec(memory_space=pl.ANY),
        out_shape=jax.ShapeDtypeStruct((total, rows, columns), pieces[0].dtype),
        scratch_shapes=[pltpu.SemaphoreType.DMA((total,))],
        cost_estimate=pl.CostEstimate(flops=0, bytes_accessed=4 * total * rows * columns, transcendentals=0),
        name="join",
    )(index, *pieces)


def tokens_kernel(*refs, counts):
    pieces = refs[: len(counts)]
    audio_ref, term_ref, other_ref, expand_ref = refs[len(counts) : len(counts) + 4]
    out_ref, weight = refs[-2:]
    at = 0
    for ref, count in zip(pieces, counts, strict=True):
        weight[at : at + count * ADAPT_SLOT] = ref[...].reshape(count * ADAPT_SLOT, ADAPT_COLS)
        at += count * ADAPT_SLOT
    pooled = (audio_ref[...] + term_ref[...] + other_ref[...].astype(jnp.float32)).astype(jnp.bfloat16)
    ordered = jnp.dot(pooled, expand_ref[...], preferred_element_type=jnp.float32).astype(jnp.bfloat16)
    out_ref[...] = jnp.dot(ordered, weight[...], preferred_element_type=jnp.float32).astype(out_ref.dtype)


def tokens_part(pieces, pooled_audio, term, other, expand, *after_these):
    counts = [p.shape[0] for p in pieces]
    count = pooled_audio.shape[0]
    whole = lambda *shape: pl.BlockSpec(shape, lambda k: (0,) * len(shape))
    return pl.pallas_call(
        functools.partial(tokens_kernel, counts=counts),
        grid=(1,),
        in_specs=[whole(n, ADAPT_SLOT, ADAPT_COLS) for n in counts]
        + [whole(*v.shape) for v in (pooled_audio, term, other, expand)]
        + [pl.BlockSpec(memory_space=pl.ANY)] * len(after_these),
        out_specs=whole(count, ADAPT_COLS),
        out_shape=jax.ShapeDtypeStruct((count, ADAPT_COLS), jnp.bfloat16),
        scratch_shapes=[pltpu.VMEM((sum(counts) * ADAPT_SLOT, ADAPT_COLS), jnp.bfloat16)],
        compiler_params=pltpu.CompilerParams(vmem_limit_bytes=VMEM),
        cost_estimate=pl.CostEstimate(
            flops=2 * count * sum(counts) * ADAPT_SLOT * (ADAPT_COLS + expand.shape[0]), bytes_accessed=8000000, transcendentals=0
        ),
        name="tokens_part",
    )(*pieces, pooled_audio, term, other, expand, *after_these)


def shards(
    audio, frame_count, ln_gain, glu_weight, dw_kernel, pw_weight, adapt_weight, text, norm_gain, qkv_weight, qkv_bias
):
    grp = lax.axis_index("grp")
    mdl = lax.axis_index("mdl")
    seq = lax.axis_index("seq")
    core, y, x = seq % 2, seq // 2 % NY, seq // (2 * NY)
    n_mdl = lax.axis_size("mdl")
    both = ("grp", "mdl")
    rows, width = adapt_weight.shape
    ring = lambda group, k: [(group * n_mdl + i, group * n_mdl + (i + k) % n_mdl) for i in range(n_mdl)]

    twin = lax.ppermute(adapt_weight, ("grp", "seq"), of_group(0, SWAP))
    held = jnp.where(
        core == 0, jnp.concatenate([adapt_weight, twin]), jnp.concatenate([twin, adapt_weight])
    )
    held = jnp.pad(held, ((0, qkv_weight.shape[0] - 2 * rows), (0, qkv_weight.shape[1] - width)))
    pieces, direct = spread(jnp.where(grp == 0, held, qkv_weight)[None])

    behind = lax.ppermute(text, both, ring(1, 1))
    ahead = lax.ppermute(text, both, ring(1, -1))
    second = lax.ppermute(behind, both, ring(1, 1))
    words = [text, ahead, second, behind]

    frames = audio.shape[0]
    gated, pooled_audio = gate(
        frame_count - seq * frames, audio, ln_gain[None], jnp.swapaxes(glu_weight, 1, 2)
    )
    up = [(i, i + 1) for i in range(lax.axis_size("seq") - 1)]
    before_edge = lax.ppermute(gated[frames - EDGE :], ("grp", "seq"), of_group(0, up))
    after_edge = lax.ppermute(gated[:EDGE], ("grp", "seq"), of_group(0, [(j, i) for i, j in up]))
    term = conv(before_edge, gated, after_edge, dw_kernel, pw_weight, pieces[0][2], behind, ahead)
    term = term.astype(jnp.float32) + lax.ppermute(
        term, both, [(0, 1), (1, 0), (2, 3), (3, 2)]
    ).astype(jnp.float32)
    other = lax.ppermute(term.astype(jnp.bfloat16), both, [(1, 2), (2, 1), (3, 0), (0, 3)])

    chips = jnp.concatenate(
        [
            jnp.stack([(x + dx) % NX * NY + (y + dy) % NY for dy in steps])
            for dx, steps, _ in pieces
        ]
    )
    column = jnp.arange(chips.shape[0] * ADAPT_SLOT, dtype=jnp.int32) % ADAPT_SLOT
    source = jnp.where(column < 2 * rows, jnp.repeat(chips, ADAPT_SLOT) * 2 * rows + column, -1)
    expand = (jnp.arange(audio.shape[1], dtype=jnp.int32)[:, None] == source[None]).astype(jnp.bfloat16)
    tokens = tokens_part([p for _, _, p in pieces[:-1]] + [direct], pooled_audio, term, other, expand, second)

    own = [p for _, _, p in pieces]
    swap = lambda v: lax.ppermute(v, ("grp", "seq"), of_group(1, SWAP))
    exchanged = [
        swap(jnp.concatenate(own[:4], axis=0)),
        swap(jnp.concatenate(own[4:7], axis=0)),
        swap(own[7]),
    ]
    index = jnp.concatenate([chips * 2 + core, chips * 2 + 1 - core])
    weight = join(index, own + exchanged).reshape(-1, qkv_weight.shape[1])

    tables = rotary_tables(2 * text.shape[0])
    gain = norm_gain.reshape(n_mdl, 1, width)
    order = (mdl + jnp.arange(n_mdl, dtype=jnp.int32)) % n_mdl
    q, kt, vt = text_part(order, words, gain, weight, qkv_bias[None], tables)
    same = lax.ppermute(tokens, both, [(i, n_mdl + i) for i in range(n_mdl)])
    following = lax.ppermute(tokens, both, [(i, n_mdl + (i - 1) % n_mdl) for i in range(n_mdl)])
    across = lax.ppermute(following, both, ring(1, -1))
    last = lax.ppermute(same, both, ring(1, 1))
    sounds = [same, following, across, last]
    context = audio_part(order, sounds, gain, weight, qkv_bias[None, -2 * HEAD :], tables, q, kt, vt)
    return jnp.where(grp == 0, tokens, context)[None]


def solution(mesh):
    in_specs = (
        P("seq", None),
        P(),
        P(),
        P(None, None, "mdl"),
        P(None, "mdl"),
        P("mdl", None),
        P("seq", "mdl"),
        P("seq", "mdl"),
        P(),
        P("seq", "mdl"),
        P("mdl"),
    )
    out_specs = P("grp", "seq", "mdl")
    return jax.shard_map(shards, mesh=mesh, in_specs=in_specs, out_specs=out_specs, check_vma=False)
```

```python
import functools

import jax
import jax.numpy as jnp
from jax import lax
from jax.experimental import pallas as pl
from jax.experimental.pallas import tpu as pltpu
from jax.sharding import PartitionSpec as P

HEADS = 28
KV = 4
HEAD = 128
VMEM = 48 * 1024 * 1024
NX = 4
NY = 8
ADAPT_SLOT = 48
ADAPT_COLS = 896


def rotary_tables(count):
    half = HEAD // 2
    freq = 1000000.0 ** (-(jnp.arange(half, dtype=jnp.float32) * 2.0 / HEAD))
    angle = jnp.arange(count, dtype=jnp.int32).astype(jnp.float32)[:, None] * freq[None, :]
    cosine, sine = jnp.cos(angle), jnp.sin(angle)
    return jnp.concatenate([cosine, cosine], 1), jnp.concatenate([-sine, sine], 1)


def turned(values, cosine, sine):
    return values * cosine + pltpu.roll(values, HEAD // 2, 1) * sine


def decode_kernel(order_ref, *refs, parts):
    words, sounds = refs[:parts], refs[parts : 2 * parts]
    gain_ref, w_ref, bias_ref, cos_ref, sin_ref, out_ref, acc, acc_kv, square, square_kv = refs[2 * parts :]
    step = pl.program_id(0)
    count, total = acc.shape
    heads = total // HEAD - 2

    @pl.when(step == 0)
    def _():
        for ref in (acc, acc_kv, square, square_kv):
            ref[...] = jnp.zeros_like(ref)

    for i in range(parts):

        @pl.when(step == i)
        def _():
            x = words[i][...].astype(jnp.float32)
            square[...] += jnp.sum(x * x, axis=1, keepdims=True)
            acc[...] += jnp.dot(
                (x * gain_ref[0]).astype(jnp.bfloat16), w_ref[...], preferred_element_type=jnp.float32
            )
            x = sounds[i][...].astype(jnp.float32)
            square_kv[...] += jnp.sum(x * x, axis=1, keepdims=True)
            acc_kv[...] += jnp.dot(
                (x * gain_ref[0]).astype(jnp.bfloat16), w_ref[:, heads * HEAD :], preferred_element_type=jnp.float32
            )

    @pl.when(step == pl.num_programs(0) - 1)
    def _():
        width = parts * words[0].shape[1]
        scale = lax.rsqrt(square[...] / width + 1e-6)
        scale_kv = lax.rsqrt(square_kv[...] / width + 1e-6)
        cosine, sine = cos_ref[count:], sin_ref[count:]
        key_cols = slice(heads * HEAD, (heads + 1) * HEAD)
        value_cols = slice((heads + 1) * HEAD, total)
        keys = jnp.concatenate(
            [
                turned(acc_kv[:, :HEAD] * scale_kv + bias_ref[:, key_cols], cos_ref[:count], sin_ref[:count]),
                turned(acc[:, key_cols] * scale + bias_ref[:, key_cols], cosine, sine),
            ],
            axis=0,
        ).astype(jnp.bfloat16)
        values = jnp.concatenate(
            [
                acc_kv[:, HEAD:] * scale_kv + bias_ref[:, value_cols],
                acc[:, value_cols] * scale + bias_ref[:, value_cols],
            ],
            axis=0,
        ).astype(jnp.bfloat16)
        row = lax.broadcasted_iota(jnp.int32, (count, 2 * count), 0)
        col = lax.broadcasted_iota(jnp.int32, (count, 2 * count), 1)
        allowed = col <= row + count
        for h in range(heads):
            cols = slice(h * HEAD, (h + 1) * HEAD)
            query = turned(acc[:, cols] * scale + bias_ref[:, cols], cosine, sine).astype(jnp.bfloat16)
            scores = lax.dot_general(
                query, keys, (((1,), (1,)), ((), ())), preferred_element_type=jnp.float32
            ) * (HEAD**-0.5)
            scores = jnp.where(allowed, scores, -1e30)
            weights = jnp.exp(scores - jnp.max(scores, axis=1, keepdims=True))
            probs = weights * (1.0 / jnp.sum(weights, axis=1, keepdims=True))
            out_ref[:, cols] = jnp.dot(
                probs.astype(jnp.bfloat16), values, preferred_element_type=jnp.float32
            ).astype(jnp.bfloat16)


def decode(order, words, sounds, gain, weight, bias, tables):
    parts = len(words)
    count, width = words[0].shape
    total = weight.shape[1]
    columns = total - 2 * HEAD
    whole = lambda *shape: pl.BlockSpec(shape, lambda k, o: (0,) * len(shape))
    return pl.pallas_call(
        functools.partial(decode_kernel, parts=parts),
        grid_spec=pltpu.PrefetchScalarGridSpec(
            num_scalar_prefetch=1,
            grid=(parts,),
            in_specs=[whole(count, width)] * (2 * parts)
            + [
                pl.BlockSpec((1, 1, width), lambda k, o: (o[k], 0, 0)),
                pl.BlockSpec((width, total), lambda k, o: (o[k], 0)),
                whole(1, total),
                whole(2 * count, HEAD),
                whole(2 * count, HEAD),
            ],
            out_specs=whole(count, columns),
            scratch_shapes=[
                pltpu.VMEM((count, total), jnp.float32),
                pltpu.VMEM((count, 2 * HEAD), jnp.float32),
                pltpu.VMEM((count, 1), jnp.float32),
                pltpu.VMEM((count, 1), jnp.float32),
            ],
        ),
        out_shape=jax.ShapeDtypeStruct((count, columns), jnp.bfloat16),
        compiler_params=pltpu.CompilerParams(vmem_limit_bytes=VMEM),
        cost_estimate=pl.CostEstimate(
            flops=2 * count * parts * width * total, bytes_accessed=2 * parts * width * (total + count), transcendentals=0
        ),
        name="decode",
    )(order, *words, *sounds, gain, weight, bias, *tables)


def pooling(rows):
    r = lax.broadcasted_iota(jnp.int32, (rows // 4, rows), 0)
    c = lax.broadcasted_iota(jnp.int32, (rows // 4, rows), 1)
    return jnp.where((c >= 4 * r) & (c < 4 * r + 4), 0.25, 0.0).astype(jnp.bfloat16)


def dot_t(a, b):
    return lax.dot_general(a, b, (((1,), (1,)), ((), ())), preferred_element_type=jnp.float32)


def gate_kernel(count_ref, audio_ref, gain_ref, weight_ref, gated_ref, pooled_ref):
    audio = audio_ref[...]
    rows = audio.astype(jnp.float32)
    centred = rows - jnp.mean(rows, axis=1, keepdims=True)
    spread = jnp.mean(centred * centred, axis=1, keepdims=True)
    normed = (centred * lax.rsqrt(spread + 1e-5) * gain_ref[...]).astype(jnp.bfloat16)
    left = dot_t(normed, weight_ref[0])
    right = dot_t(normed, weight_ref[1])
    frame = pl.program_id(0) * rows.shape[0] + lax.broadcasted_iota(jnp.int32, (rows.shape[0], 1), 0)
    gated = left * (1.0 / (1.0 + jnp.exp(-right)))
    gated_ref[...] = jnp.where(frame < count_ref[0], gated, 0.0).astype(gated_ref.dtype)
    pooled_ref[...] = jnp.dot(pooling(rows.shape[0]), audio, preferred_element_type=jnp.float32)


def gate(left_frames, audio, gain, weight):
    frames, width = audio.shape
    columns = weight.shape[1]
    block = 256
    return pl.pallas_call(
        gate_kernel,
        grid=(frames // block,),
        in_specs=[
            pl.BlockSpec(memory_space=pltpu.SMEM),
            pl.BlockSpec((block, width), lambda i: (i, 0)),
            pl.BlockSpec((1, width), lambda i: (0, 0)),
            pl.BlockSpec((2, columns, width), lambda i: (0, 0, 0)),
        ],
        out_specs=[
            pl.BlockSpec((block, columns), lambda i: (i, 0)),
            pl.BlockSpec((block // 4, width), lambda i: (i, 0)),
        ],
        out_shape=[
            jax.ShapeDtypeStruct((frames, columns), jnp.bfloat16),
            jax.ShapeDtypeStruct((frames // 4, width), jnp.float32),
        ],
        compiler_params=pltpu.CompilerParams(vmem_limit_bytes=VMEM),
        cost_estimate=pl.CostEstimate(
            flops=4 * frames * width * columns, bytes_accessed=2 * frames * width * 4, transcendentals=frames * columns
        ),
        name="gate",
    )(left_frames, audio, gain, weight)


EDGE = 16


def conv_kernel(before_ref, gated_ref, after_ref, taps_ref, pw_ref, *refs):
    term_ref, padded, act = refs[-3:]
    frames, columns = gated_ref.shape
    taps = taps_ref.shape[0]
    padded[:EDGE] = before_ref[...].astype(jnp.float32)
    padded[EDGE : EDGE + frames] = gated_ref[...].astype(jnp.float32)
    padded[EDGE + frames :] = after_ref[...].astype(jnp.float32)
    chunk = 64
    lead = EDGE - (taps - 1) // 2
    for at in range(0, columns, 128):
        lanes = slice(at, min(at + 128, columns))

        def body(i, carry, lanes=lanes):
            first = pl.multiple_of(i * chunk, chunk)
            window = padded[pl.ds(first, chunk + 2 * EDGE), lanes]
            total = jnp.zeros((chunk, window.shape[1]), jnp.float32)
            for turn in range(8):
                turned_by = window if turn == 0 else pltpu.roll(window, window.shape[0] - turn, 0)
                for offset in range(turn, lead + taps, 8):
                    if offset >= lead:
                        start = offset - turn
                        total = total + turned_by[start : start + chunk] * taps_ref[offset - lead, lanes][None]
            value = total * (1.0 / (1.0 + jnp.exp(-total)))
            act[pl.ds(first, chunk), lanes] = value.astype(jnp.bfloat16)
            return carry

        lax.fori_loop(0, frames // chunk, body, 0)
    pooled = jnp.dot(pooling(frames), act[...], preferred_element_type=jnp.float32).astype(jnp.bfloat16)
    term_ref[...] = jnp.dot(pooled, pw_ref[...], preferred_element_type=jnp.float32).astype(term_ref.dtype)


def conv(before, gated, after, taps, pw, *after_these):
    frames, columns = gated.shape
    vmem = pl.BlockSpec(memory_space=pltpu.VMEM)
    return pl.pallas_call(
        conv_kernel,
        in_specs=[vmem] * 5 + [pl.BlockSpec(memory_space=pl.ANY)] * len(after_these),
        out_specs=vmem,
        out_shape=jax.ShapeDtypeStruct((frames // 4, pw.shape[1]), jnp.bfloat16),
        scratch_shapes=[
            pltpu.VMEM((frames + 2 * EDGE, columns), jnp.float32),
            pltpu.VMEM((frames, columns), jnp.bfloat16),
        ],
        compiler_params=pltpu.CompilerParams(vmem_limit_bytes=VMEM),
        cost_estimate=pl.CostEstimate(
            flops=5_000_000_000, bytes_accessed=2 * frames * columns * 4, transcendentals=frames * columns
        ),
        name="conv",
    )(before, gated, after, taps, pw, *after_these)


def place(shift_x, shift_y):
    return [
        ((x * NY + y) * 2 + c, ((x + shift_x) % NX * NY + (y + shift_y) % NY) * 2 + c)
        for x in range(NX)
        for y in range(NY)
        for c in range(2)
    ]


SWAP = [(i, i ^ 1) for i in range(NX * NY * 2)]


def of_group(group, pairs):
    count = NX * NY * 2
    return [(group * count + i, group * count + j) for i, j in pairs]


def spread(block):
    send = lambda v, dx, dy: lax.ppermute(v, ("grp", "seq"), of_group(0, place(dx, dy)))
    near = jnp.concatenate([send(block, 0, 1), block, send(block, 0, -1)], axis=0)
    line = jnp.concatenate([near, send(near, 0, 3), send(near[:2], 0, -3)], axis=0)
    steps = [-1, 0, 1, -4, -3, -2, 2, 3]
    return [(0, steps, line)] + [(dx, steps, send(line, -dx, 0)) for dx in (-1, 1, 2)]


def tokens_kernel(*refs, counts):
    pieces = refs[: len(counts)]
    audio_ref, term_ref, other_ref, expand_ref = refs[len(counts) : len(counts) + 4]
    out_ref, weight = refs[-2:]
    at = 0
    for ref, count in zip(pieces, counts, strict=True):
        weight[at : at + count * ADAPT_SLOT] = ref[...].reshape(count * ADAPT_SLOT, ADAPT_COLS)
        at += count * ADAPT_SLOT
    pooled = (audio_ref[...] + term_ref[...] + other_ref[...].astype(jnp.float32)).astype(jnp.bfloat16)
    ordered = jnp.dot(pooled, expand_ref[...], preferred_element_type=jnp.float32).astype(jnp.bfloat16)
    out_ref[...] = jnp.dot(ordered, weight[...], preferred_element_type=jnp.float32).astype(out_ref.dtype)


def tokens_part(pieces, pooled_audio, term, other, expand, *after_these):
    counts = [p.shape[0] for p in pieces]
    count = pooled_audio.shape[0]
    whole = lambda *shape: pl.BlockSpec(shape, lambda k: (0,) * len(shape))
    return pl.pallas_call(
        functools.partial(tokens_kernel, counts=counts),
        grid=(1,),
        in_specs=[whole(n, ADAPT_SLOT, ADAPT_COLS) for n in counts]
        + [whole(*v.shape) for v in (pooled_audio, term, other, expand)]
        + [pl.BlockSpec(memory_space=pl.ANY)] * len(after_these),
        out_specs=whole(count, ADAPT_COLS),
        out_shape=jax.ShapeDtypeStruct((count, ADAPT_COLS), jnp.bfloat16),
        scratch_shapes=[pltpu.VMEM((sum(counts) * ADAPT_SLOT, ADAPT_COLS), jnp.bfloat16)],
        compiler_params=pltpu.CompilerParams(vmem_limit_bytes=VMEM),
        cost_estimate=pl.CostEstimate(
            flops=2 * count * sum(counts) * ADAPT_SLOT * (ADAPT_COLS + expand.shape[0]), bytes_accessed=8000000, transcendentals=0
        ),
        name="tokens_part",
    )(*pieces, pooled_audio, term, other, expand, *after_these)


def shards(
    audio, frame_count, ln_gain, glu_weight, dw_kernel, pw_weight, adapt_weight, text, norm_gain, qkv_weight, qkv_bias
):
    grp = lax.axis_index("grp")
    mdl = lax.axis_index("mdl")
    seq = lax.axis_index("seq")
    core, y, x = seq % 2, seq // 2 % NY, seq // (2 * NY)
    n_mdl = lax.axis_size("mdl")
    both = ("grp", "mdl")
    rows, width = adapt_weight.shape
    ring = lambda group, k: [(group * n_mdl + i, group * n_mdl + (i + k) % n_mdl) for i in range(n_mdl)]

    weight = lax.all_gather(qkv_weight, "seq", axis=0, tiled=True)
    twin = lax.ppermute(adapt_weight, ("grp", "seq"), of_group(0, SWAP))
    held = jnp.where(
        core == 0, jnp.concatenate([adapt_weight, twin]), jnp.concatenate([twin, adapt_weight])
    )
    pieces = spread(jnp.pad(held, ((0, ADAPT_SLOT - 2 * rows), (0, 0)))[None])

    behind = lax.ppermute(text, both, ring(1, 1))
    ahead = lax.ppermute(text, both, ring(1, -1))
    second = lax.ppermute(behind, both, ring(1, 1))
    words = [text, ahead, second, behind]

    frames = audio.shape[0]
    gated, pooled_audio = gate(
        frame_count - seq * frames, audio, ln_gain[None], jnp.swapaxes(glu_weight, 1, 2)
    )
    up = [(i, i + 1) for i in range(lax.axis_size("seq") - 1)]
    before_edge = lax.ppermute(gated[frames - EDGE :], ("grp", "seq"), of_group(0, up))
    after_edge = lax.ppermute(gated[:EDGE], ("grp", "seq"), of_group(0, [(j, i) for i, j in up]))
    term = conv(before_edge, gated, after_edge, dw_kernel, pw_weight, behind, ahead)
    term = term.astype(jnp.float32) + lax.ppermute(
        term, both, [(0, 1), (1, 0), (2, 3), (3, 2)]
    ).astype(jnp.float32)
    other = lax.ppermute(term.astype(jnp.bfloat16), both, [(1, 2), (2, 1), (3, 0), (0, 3)])

    chips = jnp.concatenate(
        [
            jnp.stack([(x + dx) % NX * NY + (y + dy) % NY for dy in steps])
            for dx, steps, _ in pieces
        ]
    )
    column = jnp.arange(chips.shape[0] * ADAPT_SLOT, dtype=jnp.int32) % ADAPT_SLOT
    source = jnp.where(column < 2 * rows, jnp.repeat(chips, ADAPT_SLOT) * 2 * rows + column, -1)
    expand = (jnp.arange(audio.shape[1], dtype=jnp.int32)[:, None] == source[None]).astype(jnp.bfloat16)
    tokens = tokens_part([p for _, _, p in pieces], pooled_audio, term, other, expand, second)

    tables = rotary_tables(2 * text.shape[0])
    gain = norm_gain.reshape(n_mdl, 1, width)
    order = (mdl + jnp.arange(n_mdl, dtype=jnp.int32)) % n_mdl
    same = lax.ppermute(tokens, both, [(i, n_mdl + i) for i in range(n_mdl)])
    following = lax.ppermute(tokens, both, [(i, n_mdl + (i - 1) % n_mdl) for i in range(n_mdl)])
    across = lax.ppermute(following, both, ring(1, -1))
    last = lax.ppermute(same, both, ring(1, 1))
    sounds = [same, following, across, last]
    context = decode(order, words, sounds, gain, weight, qkv_bias[None], tables)
    return jnp.where(grp == 0, tokens, context)[None]


def solution(mesh):
    in_specs = (
        P("seq", None),
        P(),
        P(),
        P(None, None, "mdl"),
        P(None, "mdl"),
        P("mdl", None),
        P("seq", "mdl"),
        P("seq", "mdl"),
        P(),
        P("seq", "mdl"),
        P("mdl"),
    )
    out_specs = P("grp", "seq", "mdl")
    return jax.shard_map(shards, mesh=mesh, in_specs=in_specs, out_specs=out_specs, check_vma=False)
```

```python
import functools

import jax
import jax.numpy as jnp
from jax import lax
from jax.experimental import pallas as pl
from jax.experimental.pallas import tpu as pltpu
from jax.sharding import Mesh
from jax.sharding import PartitionSpec as P

HEADS = 28
KV = 4
HEAD = 128
VMEM = 48 * 1024 * 1024
NX = 4
NY = 8
SEQ = ("x", "y", "core")


def rotary_tables(count):
    half = HEAD // 2
    freq = 1000000.0 ** (-(jnp.arange(half, dtype=jnp.float32) * 2.0 / HEAD))
    angle = jnp.arange(count, dtype=jnp.int32).astype(jnp.float32)[:, None] * freq[None, :]
    cosine, sine = jnp.cos(angle), jnp.sin(angle)
    return jnp.concatenate([cosine, cosine], 1), jnp.concatenate([-sine, sine], 1)


def turned(values, cosine, sine):
    return values * cosine + pltpu.roll(values, HEAD // 2, 1) * sine


def decode_kernel(order_ref, *refs, parts):
    words, sounds, line, halves = refs[:parts], refs[parts : 2 * parts], refs[2 * parts], refs[2 * parts + 1 : 4 * parts - 1]
    gain_ref, bias_ref, cos_ref, sin_ref, out_ref, rows, weight, acc, acc_kv, square, square_kv, sem = refs[4 * parts - 1 :]
    count, total = acc.shape
    heads = total // HEAD - 2
    depth = weight.shape[1]
    core = order_ref[2 * parts]
    copies = [[pltpu.make_async_copy(line, weight.at[0], sem.at[0])]]
    for i in range(parts - 1):
        pair = []
        for j in range(2):
            first = pl.multiple_of((core if j == 0 else 1 - core) * (depth // 2), depth // 2)
            at = 1 + 2 * i + j
            pair.append(
                pltpu.make_async_copy(halves[2 * i + j], weight.at[i + 1, pl.ds(first, depth // 2)], sem.at[at])
            )
        copies.append(pair)
    for pair in copies:
        for copy in pair:
            copy.start()
    square[...] = jnp.zeros_like(square)
    square_kv[...] = jnp.zeros_like(square_kv)
    for i in range(parts):
        block = order_ref[i]
        for ref, total_square, first in ((words[i], square, 0), (sounds[i], square_kv, count)):
            x = ref[...].astype(jnp.float32)
            total_square[...] += jnp.sum(x * x, axis=1, keepdims=True)
            rows[block, first : first + count] = (x * gain_ref[block]).astype(jnp.bfloat16)
    for i in range(parts):
        block = order_ref[parts + i]
        for copy in copies[i]:
            copy.wait()
        term = jnp.dot(rows[block, :count], weight[i], preferred_element_type=jnp.float32)
        term_kv = jnp.dot(rows[block, count:], weight[i, :, heads * HEAD :], preferred_element_type=jnp.float32)
        acc[...] = term if i == 0 else acc[...] + term
        acc_kv[...] = term_kv if i == 0 else acc_kv[...] + term_kv
    width = parts * depth
    scale = lax.rsqrt(square[...] / width + 1e-6)
    scale_kv = lax.rsqrt(square_kv[...] / width + 1e-6)
    cosine, sine = cos_ref[count:], sin_ref[count:]
    key_cols = slice(heads * HEAD, (heads + 1) * HEAD)
    value_cols = slice((heads + 1) * HEAD, total)
    keys = jnp.concatenate(
        [
            turned(acc_kv[:, :HEAD] * scale_kv + bias_ref[:, key_cols], cos_ref[:count], sin_ref[:count]),
            turned(acc[:, key_cols] * scale + bias_ref[:, key_cols], cosine, sine),
        ],
        axis=0,
    ).astype(jnp.bfloat16)
    values = jnp.concatenate(
        [
            acc_kv[:, HEAD:] * scale_kv + bias_ref[:, value_cols],
            acc[:, value_cols] * scale + bias_ref[:, value_cols],
        ],
        axis=0,
    ).astype(jnp.bfloat16)
    row = lax.broadcasted_iota(jnp.int32, (count, 2 * count), 0)
    col = lax.broadcasted_iota(jnp.int32, (count, 2 * count), 1)
    allowed = col <= row + count
    for h in range(heads):
        cols = slice(h * HEAD, (h + 1) * HEAD)
        query = turned(acc[:, cols] * scale + bias_ref[:, cols], cosine, sine).astype(jnp.bfloat16)
        scores = lax.dot_general(
            query, keys, (((1,), (1,)), ((), ())), preferred_element_type=jnp.float32
        ) * (HEAD**-0.5)
        scores = jnp.where(allowed, scores, -1e30)
        weights = jnp.exp(scores - jnp.max(scores, axis=1, keepdims=True))
        probs = weights * (1.0 / jnp.sum(weights, axis=1, keepdims=True))
        out_ref[:, cols] = jnp.dot(
            probs.astype(jnp.bfloat16), values, preferred_element_type=jnp.float32
        ).astype(jnp.bfloat16)


def decode(order, words, sounds, line, halves, gain, bias, tables):
    parts = len(words)
    count, width = words[0].shape
    total = line.shape[1]
    columns = total - 2 * HEAD
    vmem = pl.BlockSpec(memory_space=pltpu.VMEM)
    anywhere = pl.BlockSpec(memory_space=pl.ANY)
    return pl.pallas_call(
        functools.partial(decode_kernel, parts=parts),
        in_specs=[pl.BlockSpec(memory_space=pltpu.SMEM)]
        + [vmem] * (2 * parts)
        + [anywhere] * (1 + len(halves))
        + [vmem] * 4,
        out_specs=vmem,
        scratch_shapes=[
            pltpu.VMEM((parts, 2 * count, width), jnp.bfloat16),
            pltpu.VMEM((parts, width, total), jnp.bfloat16),
            pltpu.VMEM((count, total), jnp.float32),
            pltpu.VMEM((count, 2 * HEAD), jnp.float32),
            pltpu.VMEM((count, 1), jnp.float32),
            pltpu.VMEM((count, 1), jnp.float32),
            pltpu.SemaphoreType.DMA((1 + len(halves),)),
        ],
        out_shape=jax.ShapeDtypeStruct((count, columns), jnp.bfloat16),
        compiler_params=pltpu.CompilerParams(vmem_limit_bytes=VMEM),
        cost_estimate=pl.CostEstimate(
            flops=2 * count * parts * width * total, bytes_accessed=2 * parts * width * (total + count), transcendentals=0
        ),
        name="decode",
    )(order, *words, *sounds, line, *halves, gain, bias, *tables)


def pooling(rows):
    r = lax.broadcasted_iota(jnp.int32, (rows // 4, rows), 0)
    c = lax.broadcasted_iota(jnp.int32, (rows // 4, rows), 1)
    return jnp.where((c >= 4 * r) & (c < 4 * r + 4), 0.25, 0.0).astype(jnp.bfloat16)


def dot_t(a, b):
    return lax.dot_general(a, b, (((1,), (1,)), ((), ())), preferred_element_type=jnp.float32)


def gate_kernel(count_ref, audio_ref, gain_ref, weight_ref, gated_ref, pooled_ref):
    audio = audio_ref[...]
    rows = audio.astype(jnp.float32)
    centred = rows - jnp.mean(rows, axis=1, keepdims=True)
    spread = jnp.mean(centred * centred, axis=1, keepdims=True)
    normed = (centred * lax.rsqrt(spread + 1e-5) * gain_ref[...]).astype(jnp.bfloat16)
    left = dot_t(normed, weight_ref[0])
    right = dot_t(normed, weight_ref[1])
    frame = pl.program_id(0) * rows.shape[0] + lax.broadcasted_iota(jnp.int32, (rows.shape[0], 1), 0)
    gated = left * (1.0 / (1.0 + jnp.exp(-right)))
    gated_ref[...] = jnp.where(frame < count_ref[0], gated, 0.0).astype(gated_ref.dtype)
    pooled_ref[...] = jnp.dot(pooling(rows.shape[0]), audio, preferred_element_type=jnp.float32)


def gate(left_frames, audio, gain, weight):
    frames, width = audio.shape
    columns = weight.shape[1]
    block = 256
    return pl.pallas_call(
        gate_kernel,
        grid=(frames // block,),
        in_specs=[
            pl.BlockSpec(memory_space=pltpu.SMEM),
            pl.BlockSpec((block, width), lambda i: (i, 0)),
            pl.BlockSpec((1, width), lambda i: (0, 0)),
            pl.BlockSpec((2, columns, width), lambda i: (0, 0, 0)),
        ],
        out_specs=[
            pl.BlockSpec((block, columns), lambda i: (i, 0)),
            pl.BlockSpec((block // 4, width), lambda i: (i, 0)),
        ],
        out_shape=[
            jax.ShapeDtypeStruct((frames, columns), jnp.bfloat16),
            jax.ShapeDtypeStruct((frames // 4, width), jnp.float32),
        ],
        compiler_params=pltpu.CompilerParams(vmem_limit_bytes=VMEM),
        cost_estimate=pl.CostEstimate(
            flops=4 * frames * width * columns, bytes_accessed=2 * frames * width * 4, transcendentals=frames * columns
        ),
        name="gate",
    )(left_frames, audio, gain, weight)


EDGE = 16


def conv_kernel(tag_ref, before_ref, gated_ref, after_ref, taps_ref, pw_ref, *refs):
    term_ref, same_ref, padded, act = refs[-4:]
    same_ref[0] = tag_ref[0]
    frames, columns = gated_ref.shape
    taps = taps_ref.shape[0]
    padded[:EDGE] = before_ref[...].astype(jnp.float32)
    padded[EDGE : EDGE + frames] = gated_ref[...].astype(jnp.float32)
    padded[EDGE + frames :] = after_ref[...].astype(jnp.float32)
    chunk = 64
    lead = EDGE - (taps - 1) // 2
    for at in range(0, columns, 128):
        lanes = slice(at, min(at + 128, columns))

        def body(i, carry, lanes=lanes):
            first = pl.multiple_of(i * chunk, chunk)
            window = padded[pl.ds(first, chunk + 2 * EDGE), lanes]
            total = jnp.zeros((chunk, window.shape[1]), jnp.float32)
            for turn in range(8):
                turned_by = window if turn == 0 else pltpu.roll(window, window.shape[0] - turn, 0)
                for offset in range(turn, lead + taps, 8):
                    if offset >= lead:
                        start = offset - turn
                        total = total + turned_by[start : start + chunk] * taps_ref[offset - lead, lanes][None]
            value = total * (1.0 / (1.0 + jnp.exp(-total)))
            act[pl.ds(first, chunk), lanes] = value.astype(jnp.bfloat16)
            return carry

        lax.fori_loop(0, frames // chunk, body, 0)
    pooled = jnp.dot(pooling(frames), act[...], preferred_element_type=jnp.float32).astype(jnp.bfloat16)
    term_ref[...] = jnp.dot(pooled, pw_ref[...], preferred_element_type=jnp.float32).astype(term_ref.dtype)


def conv(tag, before, gated, after, taps, pw, *after_these):
    frames, columns = gated.shape
    vmem = pl.BlockSpec(memory_space=pltpu.VMEM)
    return pl.pallas_call(
        conv_kernel,
        in_specs=[pl.BlockSpec(memory_space=pltpu.SMEM)]
        + [vmem] * 5
        + [pl.BlockSpec(memory_space=pl.ANY)] * len(after_these),
        out_specs=[vmem, pl.BlockSpec(memory_space=pltpu.SMEM)],
        out_shape=[
            jax.ShapeDtypeStruct((frames // 4, pw.shape[1]), jnp.bfloat16),
            jax.ShapeDtypeStruct((1,), jnp.int32),
        ],
        scratch_shapes=[
            pltpu.VMEM((frames + 2 * EDGE, columns), jnp.float32),
            pltpu.VMEM((frames, columns), jnp.bfloat16),
        ],
        compiler_params=pltpu.CompilerParams(vmem_limit_bytes=VMEM),
        cost_estimate=pl.CostEstimate(
            flops=5_000_000_000, bytes_accessed=2 * frames * columns * 4, transcendentals=frames * columns
        ),
        name="conv",
    )(tag, before, gated, after, taps, pw, *after_these)


def place(shift_x, shift_y):
    return [
        ((x * NY + y) * 2 + c, ((x + shift_x) % NX * NY + (y + shift_y) % NY) * 2 + c)
        for x in range(NX)
        for y in range(NY)
        for c in range(2)
    ]


SWAP = [(i, i ^ 1) for i in range(NX * NY * 2)]


def of_group(group, pairs):
    count = NX * NY * 2
    return [(group * count + i, group * count + j) for i, j in pairs]


def tokens_kernel(at_ref, *refs, counts):
    pieces = refs[: len(counts)]
    audio_ref, term_ref, other_ref = refs[len(counts) : len(counts) + 3]
    out_ref, weight = refs[-2:]
    run = min(counts)
    at = 0
    for ref, count in zip(pieces, counts, strict=True):
        for first in range(0, count, run):
            weight[pl.ds(pl.multiple_of(at_ref[at] * run, run), run)] = ref[first : first + run]
            at += 1
    pooled = (audio_ref[...] + term_ref[...] + other_ref[...].astype(jnp.float32)).astype(jnp.bfloat16)
    out_ref[...] = jnp.dot(pooled, weight[...], preferred_element_type=jnp.float32).astype(out_ref.dtype)


def tokens_part(at, pieces, pooled_audio, term, other, *after_these):
    counts = [p.shape[0] for p in pieces]
    count = pooled_audio.shape[0]
    columns = pieces[0].shape[1]
    vmem = pl.BlockSpec(memory_space=pltpu.VMEM)
    return pl.pallas_call(
        functools.partial(tokens_kernel, counts=counts),
        in_specs=[pl.BlockSpec(memory_space=pltpu.SMEM)]
        + [vmem] * (len(pieces) + 3)
        + [pl.BlockSpec(memory_space=pl.ANY)] * len(after_these),
        out_specs=vmem,
        out_shape=jax.ShapeDtypeStruct((count, columns), jnp.bfloat16),
        scratch_shapes=[pltpu.VMEM((sum(counts), columns), jnp.bfloat16)],
        compiler_params=pltpu.CompilerParams(vmem_limit_bytes=VMEM),
        cost_estimate=pl.CostEstimate(
            flops=2 * count * sum(counts) * columns, bytes_accessed=8000000, transcendentals=0
        ),
        name="tokens_part",
    )(at, *pieces, pooled_audio, term, other, *after_these)


def shards(
    audio, frame_count, ln_gain, glu_weight, dw_kernel, pw_weight, adapt_weight, text, norm_gain, qkv_weight, qkv_bias
):
    grp = lax.axis_index("grp")
    mdl = lax.axis_index("mdl")
    x, core = lax.axis_index("x"), lax.axis_index("core")
    seq = lax.axis_index(SEQ)
    n_mdl = lax.axis_size("mdl")
    both = ("grp", "mdl")
    rows, width = adapt_weight.shape
    ring = lambda group, k: [(group * n_mdl + i, group * n_mdl + (i + k) % n_mdl) for i in range(n_mdl)]

    held = jnp.pad(adapt_weight, ((0, qkv_weight.shape[0] - rows), (0, qkv_weight.shape[1] - width)))
    line = lax.all_gather(jnp.where(grp == 0, held, qkv_weight), ("y", "core"), axis=0, tiled=True)
    send = lambda group, v, pairs: lax.ppermute(v, ("grp",) + SEQ, of_group(group, pairs))
    behind = lax.ppermute(text, both, ring(1, 1))
    ahead = lax.ppermute(text, both, ring(1, -1))
    second = lax.ppermute(behind, both, ring(1, 1))
    words = [text, ahead, second, behind]

    frames = audio.shape[0]
    gated, pooled_audio = gate(
        frame_count - seq * frames, audio, ln_gain[None], jnp.swapaxes(glu_weight, 1, 2)
    )
    up = [(i, i + 1) for i in range(2 * NX * NY - 1)]
    before_edge = send(0, gated[frames - EDGE :], up)
    after_edge = send(0, gated[:EDGE], [(j, i) for i, j in up])
    term, turn = conv(core[None], before_edge, gated, after_edge, dw_kernel, pw_weight, behind, ahead)
    turn = turn[0]
    adapter = line.reshape(2 * NY, -1, line.shape[1])[:, :rows, :width].reshape(2 * NY * rows, width)
    half = lax.dynamic_slice_in_dim(adapter, turn * (NY * rows), NY * rows)
    adapter_far = [send(0, half, place(-dx, 0)) for dx in (-1, 1, 2)]
    adapter_twin = send(0, jnp.concatenate(adapter_far), SWAP)

    depth = line.shape[0] // 2
    half = lax.dynamic_slice_in_dim(line, turn * depth, depth)
    from_behind = send(1, half, place(1, 0))
    from_ahead = send(1, half, place(-1, 0))
    from_across = jnp.concatenate(
        [
            send(1, from_behind[: depth // 2], place(1, 0)),
            send(1, from_ahead[depth // 2 :], place(-1, 0)),
        ]
    )
    halves = []
    for piece in (from_behind, from_ahead, from_across):
        halves += [piece, send(1, piece, SWAP)]

    term = term.astype(jnp.float32) + lax.ppermute(
        term, both, [(0, 1), (1, 0), (2, 3), (3, 2)]
    ).astype(jnp.float32)
    other = lax.ppermute(term.astype(jnp.bfloat16), both, [(1, 2), (2, 1), (3, 0), (0, 3)])

    far = [(x - 1) % NX, (x + 1) % NX, (x + 2) % NX]
    at = [2 * x, 2 * x + 1] + [2 * i + core for i in far] + [2 * i + 1 - core for i in far]
    tokens = tokens_part(
        jnp.stack(at), [adapter] + adapter_far + [adapter_twin], pooled_audio, term, other, second
    )

    tables = rotary_tables(2 * text.shape[0])
    gain = norm_gain.reshape(n_mdl, 1, width)
    order = jnp.stack([(mdl + i) % n_mdl for i in range(n_mdl)] + [x] + far + [core])
    same = lax.ppermute(tokens, both, [(i, n_mdl + i) for i in range(n_mdl)])
    following = lax.ppermute(tokens, both, [(i, n_mdl + (i - 1) % n_mdl) for i in range(n_mdl)])
    across = lax.ppermute(following, both, ring(1, -1))
    last = lax.ppermute(same, both, ring(1, 1))
    sounds = [same, following, across, last]
    context = decode(order, words, sounds, line, halves, gain, qkv_bias[None], tables)
    return jnp.where(grp == 0, tokens, context)[None]


def solution(mesh):
    mesh = Mesh(
        mesh.devices.reshape(mesh.shape["grp"], NX, NY, 2, mesh.shape["mdl"]), ("grp", *SEQ, "mdl")
    )
    in_specs = (
        P(SEQ, None),
        P(),
        P(),
        P(None, None, "mdl"),
        P(None, "mdl"),
        P("mdl", None),
        P(SEQ, "mdl"),
        P(SEQ, "mdl"),
        P(),
        P(SEQ, "mdl"),
        P("mdl"),
    )
    out_specs = P("grp", SEQ, "mdl")
    return jax.shard_map(shards, mesh=mesh, in_specs=in_specs, out_specs=out_specs, check_vma=False)
```

```python
import functools

import jax
import jax.numpy as jnp
from jax import lax
from jax.experimental import pallas as pl
from jax.experimental.pallas import tpu as pltpu
from jax.sharding import PartitionSpec as P

HEADS = 28
KV = 4
HEAD = 128
MIB = 1024 * 1024
LOG2E = 1.4426950408889634
NX = 4
NY = 8


def rotary_tables(count):
    half = HEAD // 2
    freq = 1000000.0 ** (-(jnp.arange(half, dtype=jnp.float32) * 2.0 / HEAD))
    angle = jnp.arange(count, dtype=jnp.int32).astype(jnp.float32)[:, None] * freq[None, :]
    cosine, sine = jnp.cos(angle), jnp.sin(angle)
    return jnp.concatenate([cosine, cosine], 1), jnp.concatenate([-sine, sine], 1)


def turned(values, cosine, sine):
    return values * cosine + pltpu.roll(values, HEAD // 2, 1) * sine


def prepare_kernel(order_ref, *refs, parts):
    ins = refs[: 2 * parts]
    gain_ref, rows_ref, scale_ref = refs[2 * parts : 2 * parts + 3]
    count = ins[0].shape[0]
    for first, blocks in ((0, ins[:parts]), (count, ins[parts:])):
        square = jnp.zeros((count, 1), jnp.float32)
        for i, ref in enumerate(blocks):
            block = order_ref[i]
            x = ref[...].astype(jnp.float32)
            square = square + jnp.sum(x * x, axis=1, keepdims=True)
            rows_ref[block, first : first + count] = (x * gain_ref[block]).astype(jnp.bfloat16)
        scale_ref[first : first + count] = lax.rsqrt(square / (parts * ins[0].shape[1]) + 1e-6)


def prepare(order, words, sounds, gain):
    parts = len(words)
    count, width = words[0].shape
    vmem = pl.BlockSpec(memory_space=pltpu.VMEM)
    return pl.pallas_call(
        functools.partial(prepare_kernel, parts=parts),
        in_specs=[pl.BlockSpec(memory_space=pltpu.SMEM)] + [vmem] * (2 * parts + 1),
        out_specs=[vmem, vmem],
        out_shape=[
            jax.ShapeDtypeStruct((parts, 2 * count, width), jnp.bfloat16),
            jax.ShapeDtypeStruct((2 * count, 1), jnp.float32),
        ],
        compiler_params=pltpu.CompilerParams(vmem_limit_bytes=16 * MIB),
        cost_estimate=pl.CostEstimate(
            flops=8 * count * parts * width, bytes_accessed=8 * count * parts * width, transcendentals=0
        ),
        name="prepare",
    )(order, *words, *sounds, gain)


def decode_kernel(rows_ref, scale_ref, w_ref, bias_ref, cos_ref, sin_ref, out_ref, acc, acc_kv):
    step = pl.program_id(0)
    count, total = acc.shape
    heads = total // HEAD - 2
    text = jnp.dot(rows_ref[0, :count], w_ref[...], preferred_element_type=jnp.float32)
    audio = jnp.dot(rows_ref[0, count:], w_ref[:, heads * HEAD :], preferred_element_type=jnp.float32)

    @pl.when(step == 0)
    def _():
        acc[...] = text
        acc_kv[...] = audio

    @pl.when(step > 0)
    def _():
        acc[...] += text
        acc_kv[...] += audio

    @pl.when(step == pl.num_programs(0) - 1)
    def _():
        scale, scale_kv = scale_ref[:count], scale_ref[count:]
        cosine, sine = cos_ref[count:], sin_ref[count:]
        key_cols = slice(heads * HEAD, (heads + 1) * HEAD)
        value_cols = slice((heads + 1) * HEAD, total)
        keys = jnp.concatenate(
            [
                turned(acc_kv[:, :HEAD] * scale_kv + bias_ref[:, key_cols], cos_ref[:count], sin_ref[:count]),
                turned(acc[:, key_cols] * scale + bias_ref[:, key_cols], cosine, sine),
            ],
            axis=0,
        ).astype(jnp.bfloat16)
        values = jnp.concatenate(
            [
                acc_kv[:, HEAD:] * scale_kv + bias_ref[:, value_cols],
                acc[:, value_cols] * scale + bias_ref[:, value_cols],
            ],
            axis=0,
        ).astype(jnp.bfloat16)
        row = lax.broadcasted_iota(jnp.int32, (count, 2 * count), 0)
        col = lax.broadcasted_iota(jnp.int32, (count, 2 * count), 1)
        allowed = col <= row + count
        for h in range(heads):
            cols = slice(h * HEAD, (h + 1) * HEAD)
            query = turned(acc[:, cols] * scale + bias_ref[:, cols], cosine, sine) * (LOG2E * HEAD**-0.5)
            scores = dot_t(query.astype(jnp.bfloat16), keys)
            scores = jnp.where(allowed, scores, -1e30)
            weights = jnp.exp2(scores - jnp.max(scores, axis=1, keepdims=True))
            probs = weights * (1.0 / jnp.sum(weights, axis=1, keepdims=True))
            out_ref[:, cols] = jnp.dot(
                probs.astype(jnp.bfloat16), values, preferred_element_type=jnp.float32
            ).astype(jnp.bfloat16)


def decode(rows, scale, weight, bias, tables):
    parts, count, width = rows.shape
    count //= 2
    total = weight.shape[1]
    columns = total - 2 * HEAD
    whole = lambda *shape: pl.BlockSpec(shape, lambda k: (0,) * len(shape))
    return pl.pallas_call(
        decode_kernel,
        grid=(parts,),
        in_specs=[
            pl.BlockSpec((1, 2 * count, width), lambda k: (k, 0, 0)),
            whole(2 * count, 1),
            pl.BlockSpec((width, total), lambda k: (k, 0)),
            whole(1, total),
            whole(2 * count, HEAD),
            whole(2 * count, HEAD),
        ],
        out_specs=whole(count, columns),
        scratch_shapes=[
            pltpu.VMEM((count, total), jnp.float32),
            pltpu.VMEM((count, 2 * HEAD), jnp.float32),
        ],
        out_shape=jax.ShapeDtypeStruct((count, columns), jnp.bfloat16),
        compiler_params=pltpu.CompilerParams(vmem_limit_bytes=56 * MIB),
        cost_estimate=pl.CostEstimate(
            flops=2 * count * parts * width * total, bytes_accessed=2 * parts * width * (total + count), transcendentals=0
        ),
        name="decode",
    )(rows, scale, weight, bias, *tables)


def pooling(rows):
    r = lax.broadcasted_iota(jnp.int32, (rows // 4, rows), 0)
    c = lax.broadcasted_iota(jnp.int32, (rows // 4, rows), 1)
    return jnp.where((c >= 4 * r) & (c < 4 * r + 4), 0.25, 0.0).astype(jnp.bfloat16)


def dot_t(a, b):
    return lax.dot_general(a, b, (((1,), (1,)), ((), ())), preferred_element_type=jnp.float32)


def gate_kernel(count_ref, audio_ref, gain_ref, weight_ref, gated_ref, pooled_ref):
    audio = audio_ref[...]
    rows = audio.astype(jnp.float32)
    centred = rows - jnp.mean(rows, axis=1, keepdims=True)
    spread = jnp.mean(centred * centred, axis=1, keepdims=True)
    normed = (centred * lax.rsqrt(spread + 1e-5) * gain_ref[...]).astype(jnp.bfloat16)
    left = dot_t(normed, weight_ref[0])
    right = dot_t(normed, weight_ref[1])
    frame = pl.program_id(0) * rows.shape[0] + lax.broadcasted_iota(jnp.int32, (rows.shape[0], 1), 0)
    gated = left * (1.0 / (1.0 + jnp.exp(-right)))
    gated_ref[...] = jnp.where(frame < count_ref[0], gated, 0.0).astype(gated_ref.dtype)
    pooled_ref[...] = jnp.dot(pooling(rows.shape[0]), audio, preferred_element_type=jnp.float32)


def gate(left_frames, audio, gain, weight):
    frames, width = audio.shape
    columns = weight.shape[1]
    block = 256
    return pl.pallas_call(
        gate_kernel,
        grid=(frames // block,),
        in_specs=[
            pl.BlockSpec(memory_space=pltpu.SMEM),
            pl.BlockSpec((block, width), lambda i: (i, 0)),
            pl.BlockSpec((1, width), lambda i: (0, 0)),
            pl.BlockSpec((2, columns, width), lambda i: (0, 0, 0)),
        ],
        out_specs=[
            pl.BlockSpec((block, columns), lambda i: (i, 0)),
            pl.BlockSpec((block // 4, width), lambda i: (i, 0)),
        ],
        out_shape=[
            jax.ShapeDtypeStruct((frames, columns), jnp.bfloat16),
            jax.ShapeDtypeStruct((frames // 4, width), jnp.float32),
        ],
        compiler_params=pltpu.CompilerParams(vmem_limit_bytes=20 * MIB),
        cost_estimate=pl.CostEstimate(
            flops=4 * frames * width * columns, bytes_accessed=2 * frames * width * 4, transcendentals=frames * columns
        ),
        name="gate",
    )(left_frames, audio, gain, weight)


EDGE = 16


def conv_kernel(before_ref, gated_ref, after_ref, taps_ref, pw_ref, *refs):
    term_ref, padded, act = refs[-3:]
    frames, columns = gated_ref.shape
    taps = taps_ref.shape[0]
    padded[:EDGE] = before_ref[...].astype(jnp.float32)
    padded[EDGE : EDGE + frames] = gated_ref[...].astype(jnp.float32)
    padded[EDGE + frames :] = after_ref[...].astype(jnp.float32)
    chunk = 64
    lead = EDGE - (taps - 1) // 2
    for at in range(0, columns, 128):
        lanes = slice(at, min(at + 128, columns))

        def body(i, carry, lanes=lanes):
            first = pl.multiple_of(i * chunk, chunk)
            window = padded[pl.ds(first, chunk + 2 * EDGE), lanes]
            total = jnp.zeros((chunk, window.shape[1]), jnp.float32)
            for turn in range(8):
                turned_by = window if turn == 0 else pltpu.roll(window, window.shape[0] - turn, 0)
                for offset in range(turn, lead + taps, 8):
                    if offset >= lead:
                        start = offset - turn
                        total = total + turned_by[start : start + chunk] * taps_ref[offset - lead, lanes][None]
            value = total * (1.0 / (1.0 + jnp.exp(-total)))
            act[pl.ds(first, chunk), lanes] = value.astype(jnp.bfloat16)
            return carry

        lax.fori_loop(0, frames // chunk, body, 0)
    pooled = jnp.dot(pooling(frames), act[...], preferred_element_type=jnp.float32).astype(jnp.bfloat16)
    term_ref[...] = jnp.dot(pooled, pw_ref[...], preferred_element_type=jnp.float32).astype(term_ref.dtype)


def conv(before, gated, after, taps, pw, *after_these):
    frames, columns = gated.shape
    vmem = pl.BlockSpec(memory_space=pltpu.VMEM)
    return pl.pallas_call(
        conv_kernel,
        in_specs=[vmem] * 5 + [pl.BlockSpec(memory_space=pl.ANY)] * len(after_these),
        out_specs=vmem,
        out_shape=jax.ShapeDtypeStruct((frames // 4, pw.shape[1]), jnp.bfloat16),
        scratch_shapes=[
            pltpu.VMEM((frames + 2 * EDGE, columns), jnp.float32),
            pltpu.VMEM((frames, columns), jnp.bfloat16),
        ],
        compiler_params=pltpu.CompilerParams(vmem_limit_bytes=12 * MIB),
        cost_estimate=pl.CostEstimate(
            flops=5_000_000_000, bytes_accessed=2 * frames * columns * 4, transcendentals=frames * columns
        ),
        name="conv",
    )(before, gated, after, taps, pw, *after_these)


def place(shift_x, shift_y):
    return [
        ((x * NY + y) * 2 + c, ((x + shift_x) % NX * NY + (y + shift_y) % NY) * 2 + c)
        for x in range(NX)
        for y in range(NY)
        for c in range(2)
    ]


SWAP = [(i, i ^ 1) for i in range(NX * NY * 2)]


def of_group(group, pairs):
    count = NX * NY * 2
    return [(group * count + i, group * count + j) for i, j in pairs]


def spread(block):
    send = lambda v, dx, dy: lax.ppermute(v, ("grp", "seq"), of_group(0, place(dx, dy)))
    rows = block.shape[0]
    near = jnp.concatenate([send(block, 0, 1), block, send(block, 0, -1)], axis=0)
    line = jnp.concatenate([near, send(near, 0, -3), send(near[rows:], 0, 3)], axis=0)
    steps = [-1, 0, 1, 2, 3, 4, -3, -2]
    return [(0, steps, line)] + [(dx, steps, send(line, -dx, 0)) for dx in (-1, 1, 2)]


def tokens_kernel(*refs, counts):
    pieces = refs[: len(counts)]
    audio_ref, term_ref, other_ref, expand_ref = refs[len(counts) : len(counts) + 4]
    out_ref, weight = refs[-2:]
    at = 0
    for ref, count in zip(pieces, counts, strict=True):
        weight[at : at + count] = ref[...]
        at += count
    pooled = (audio_ref[...] + term_ref[...] + other_ref[...].astype(jnp.float32)).astype(jnp.bfloat16)
    ordered = jnp.dot(pooled, expand_ref[...], preferred_element_type=jnp.float32).astype(jnp.bfloat16)
    out_ref[...] = jnp.dot(ordered, weight[...], preferred_element_type=jnp.float32).astype(out_ref.dtype)


def tokens_part(pieces, pooled_audio, term, other, expand, *after_these):
    counts = [p.shape[0] for p in pieces]
    count = pooled_audio.shape[0]
    columns = pieces[0].shape[1]
    vmem = pl.BlockSpec(memory_space=pltpu.VMEM)
    return pl.pallas_call(
        functools.partial(tokens_kernel, counts=counts),
        in_specs=[vmem] * (len(pieces) + 4) + [pl.BlockSpec(memory_space=pl.ANY)] * len(after_these),
        out_specs=vmem,
        out_shape=jax.ShapeDtypeStruct((count, columns), jnp.bfloat16),
        scratch_shapes=[pltpu.VMEM((sum(counts), columns), jnp.bfloat16)],
        compiler_params=pltpu.CompilerParams(vmem_limit_bytes=20 * MIB),
        cost_estimate=pl.CostEstimate(
            flops=4 * count * sum(counts) * columns, bytes_accessed=8000000, transcendentals=0
        ),
        name="tokens_part",
    )(*pieces, pooled_audio, term, other, expand, *after_these)


def shards(
    audio, frame_count, ln_gain, glu_weight, dw_kernel, pw_weight, adapt_weight, text, norm_gain, qkv_weight, qkv_bias
):
    grp = lax.axis_index("grp")
    mdl = lax.axis_index("mdl")
    seq = lax.axis_index("seq")
    core, y, x = seq % 2, seq // 2 % NY, seq // (2 * NY)
    n_mdl = lax.axis_size("mdl")
    both = ("grp", "mdl")
    rows, width = adapt_weight.shape
    ring = lambda group, k: [(group * n_mdl + i, group * n_mdl + (i + k) % n_mdl) for i in range(n_mdl)]

    weight = lax.all_gather(qkv_weight, "seq", axis=0, tiled=True)
    pieces = spread(adapt_weight)
    swap = lambda v: lax.ppermute(v, ("grp", "seq"), of_group(0, SWAP))
    adapter = [p for _, _, p in pieces]
    adapter += [swap(adapter[0]), swap(jnp.concatenate(adapter[1:], axis=0))]

    behind = lax.ppermute(text, both, ring(1, 1))
    ahead = lax.ppermute(text, both, ring(1, -1))
    second = lax.ppermute(behind, both, ring(1, 1))
    words = [text, ahead, second, behind]

    frames = audio.shape[0]
    gated, pooled_audio = gate(
        frame_count - seq * frames, audio, ln_gain[None], jnp.swapaxes(glu_weight, 1, 2)
    )
    up = [(i, i + 1) for i in range(lax.axis_size("seq") - 1)]
    before_edge = lax.ppermute(gated[frames - EDGE :], ("grp", "seq"), of_group(0, up))
    after_edge = lax.ppermute(gated[:EDGE], ("grp", "seq"), of_group(0, [(j, i) for i, j in up]))
    term = conv(before_edge, gated, after_edge, dw_kernel, pw_weight, behind, ahead)
    term = term.astype(jnp.float32) + lax.ppermute(
        term, both, [(0, 1), (1, 0), (2, 3), (3, 2)]
    ).astype(jnp.float32)
    other = lax.ppermute(term.astype(jnp.bfloat16), both, [(1, 2), (2, 1), (3, 0), (0, 3)])

    chips = jnp.concatenate(
        [
            jnp.stack([(x + dx) % NX * NY + (y + dy) % NY for dy in steps])
            for dx, steps, _ in pieces
        ]
    )
    device = jnp.concatenate([2 * chips + core, 2 * chips + 1 - core])
    source = (device[:, None] * rows + jnp.arange(rows, dtype=jnp.int32)[None]).reshape(-1)
    expand = (jnp.arange(audio.shape[1], dtype=jnp.int32)[:, None] == source[None]).astype(jnp.bfloat16)
    tokens = tokens_part(adapter, pooled_audio, term, other, expand, second)

    tables = rotary_tables(2 * text.shape[0])
    gain = norm_gain.reshape(n_mdl, 1, width)
    order = (mdl + jnp.arange(n_mdl, dtype=jnp.int32)) % n_mdl
    same = lax.ppermute(tokens, both, [(i, n_mdl + i) for i in range(n_mdl)])
    following = lax.ppermute(tokens, both, [(i, n_mdl + (i - 1) % n_mdl) for i in range(n_mdl)])
    across = lax.ppermute(following, both, ring(1, -1))
    last = lax.ppermute(same, both, ring(1, 1))
    sounds = [same, following, across, last]
    prepared, scale = prepare(order, words, sounds, gain)
    context = decode(prepared, scale, weight, qkv_bias[None], tables)
    return jnp.where(grp == 0, tokens, context)[None]


def solution(mesh):
    in_specs = (
        P("seq", None),
        P(),
        P(),
        P(None, None, "mdl"),
        P(None, "mdl"),
        P("mdl", None),
        P("seq", "mdl"),
        P("seq", "mdl"),
        P(),
        P("seq", "mdl"),
        P("mdl"),
    )
    out_specs = P("grp", "seq", "mdl")
    return jax.shard_map(shards, mesh=mesh, in_specs=in_specs, out_specs=out_specs, check_vma=False)
```

```python
import functools

import jax
import jax.numpy as jnp
from jax import lax
from jax.experimental import pallas as pl
from jax.experimental.pallas import tpu as pltpu
from jax.sharding import PartitionSpec as P

HEADS = 28
KV = 4
HEAD = 128
MIB = 1024 * 1024
LOG2E = 1.4426950408889634
NX = 4
NY = 8


def rotary_tables(count):
    half = HEAD // 2
    freq = 1000000.0 ** (-(jnp.arange(half, dtype=jnp.float32) * 2.0 / HEAD))
    angle = jnp.arange(count, dtype=jnp.int32).astype(jnp.float32)[:, None] * freq[None, :]
    cosine, sine = jnp.cos(angle), jnp.sin(angle)
    return jnp.concatenate([cosine, cosine], 1), jnp.concatenate([-sine, sine], 1)


def turned(values, cosine, sine):
    return values * cosine + pltpu.roll(values, HEAD // 2, 1) * sine


def decode_kernel(
    order_ref, *refs, parts
):
    ins = refs[: 2 * parts]
    gain_ref, w_ref, bias_ref, cos_ref, sin_ref, out_ref, held, rows, scales, acc, acc_kv, sem = refs[2 * parts :]
    step = pl.program_id(0)
    count, total = acc.shape
    heads = total // HEAD - 2
    width = held.shape[2]

    @pl.when(step == 0)
    def _():
        copies = [pltpu.make_async_copy(ref, held.at[i], sem.at[i]) for i, ref in enumerate(ins)]
        for copy in copies:
            copy.start()
        for first, side in ((0, 0), (count, parts)):
            square = jnp.zeros((count, 1), jnp.float32)
            for i in range(parts):
                copies[side + i].wait()
                block = order_ref[i]
                x = held[side + i].astype(jnp.float32)
                square = square + jnp.sum(x * x, axis=1, keepdims=True)
                rows[block, first : first + count] = (x * gain_ref[block]).astype(jnp.bfloat16)
            scales[first : first + count] = lax.rsqrt(square / (parts * width) + 1e-6)

    text = jnp.dot(rows[step, :count], w_ref[...], preferred_element_type=jnp.float32)
    audio = jnp.dot(rows[step, count:], w_ref[:, heads * HEAD :], preferred_element_type=jnp.float32)

    @pl.when(step == 0)
    def _():
        acc[...] = text
        acc_kv[...] = audio

    @pl.when(step > 0)
    def _():
        acc[...] += text
        acc_kv[...] += audio

    @pl.when(step == pl.num_programs(0) - 1)
    def _():
        scale, scale_kv = scales[:count], scales[count:]
        cosine, sine = cos_ref[count:], sin_ref[count:]
        key_cols = slice(heads * HEAD, (heads + 1) * HEAD)
        value_cols = slice((heads + 1) * HEAD, total)
        keys = jnp.concatenate(
            [
                turned(acc_kv[:, :HEAD] * scale_kv + bias_ref[:, key_cols], cos_ref[:count], sin_ref[:count]),
                turned(acc[:, key_cols] * scale + bias_ref[:, key_cols], cosine, sine),
            ],
            axis=0,
        ).astype(jnp.bfloat16)
        values = jnp.concatenate(
            [
                acc_kv[:, HEAD:] * scale_kv + bias_ref[:, value_cols],
                acc[:, value_cols] * scale + bias_ref[:, value_cols],
            ],
            axis=0,
        ).astype(jnp.bfloat16)
        row = lax.broadcasted_iota(jnp.int32, (count, 2 * count), 0)
        col = lax.broadcasted_iota(jnp.int32, (count, 2 * count), 1)
        allowed = col <= row + count
        for h in range(heads):
            cols = slice(h * HEAD, (h + 1) * HEAD)
            query = turned(acc[:, cols] * scale + bias_ref[:, cols], cosine, sine) * (LOG2E * HEAD**-0.5)
            scores = dot_t(query.astype(jnp.bfloat16), keys)
            scores = jnp.where(allowed, scores, -1e30)
            weights = jnp.exp2(scores - jnp.max(scores, axis=1, keepdims=True))
            probs = weights * (1.0 / jnp.sum(weights, axis=1, keepdims=True))
            out_ref[:, cols] = jnp.dot(
                probs.astype(jnp.bfloat16), values, preferred_element_type=jnp.float32
            ).astype(jnp.bfloat16)


def decode(order, words, sounds, gain, weight, bias, tables):
    parts = len(words)
    count, width = words[0].shape
    total = weight.shape[1]
    columns = total - 2 * HEAD
    whole = lambda *shape: pl.BlockSpec(shape, lambda k: (0,) * len(shape))
    return pl.pallas_call(
        functools.partial(decode_kernel, parts=parts),
        grid=(parts,),
        in_specs=[pl.BlockSpec(memory_space=pltpu.SMEM)]
        + [pl.BlockSpec(memory_space=pl.ANY)] * (2 * parts)
        + [
            whole(parts, 1, width),
            pl.BlockSpec((width, total), lambda k: (k, 0)),
            whole(1, total),
            whole(2 * count, HEAD),
            whole(2 * count, HEAD),
        ],
        out_specs=whole(count, columns),
        scratch_shapes=[
            pltpu.VMEM((2 * parts, count, width), jnp.bfloat16),
            pltpu.VMEM((parts, 2 * count, width), jnp.bfloat16),
            pltpu.VMEM((2 * count, 1), jnp.float32),
            pltpu.VMEM((count, total), jnp.float32),
            pltpu.VMEM((count, 2 * HEAD), jnp.float32),
            pltpu.SemaphoreType.DMA((2 * parts,)),
        ],
        out_shape=jax.ShapeDtypeStruct((count, columns), jnp.bfloat16),
        compiler_params=pltpu.CompilerParams(vmem_limit_bytes=56 * MIB),
        cost_estimate=pl.CostEstimate(
            flops=2 * count * parts * width * total, bytes_accessed=2 * parts * width * (total + count), transcendentals=0
        ),
        name="decode",
    )(order, *words, *sounds, gain, weight, bias, *tables)


def pooling(rows):
    r = lax.broadcasted_iota(jnp.int32, (rows // 4, rows), 0)
    c = lax.broadcasted_iota(jnp.int32, (rows // 4, rows), 1)
    return jnp.where((c >= 4 * r) & (c < 4 * r + 4), 0.25, 0.0).astype(jnp.bfloat16)


def dot_t(a, b):
    return lax.dot_general(a, b, (((1,), (1,)), ((), ())), preferred_element_type=jnp.float32)


def gate_kernel(count_ref, audio_ref, gain_ref, weight_ref, gated_ref, pooled_ref):
    audio = audio_ref[...]
    rows = audio.astype(jnp.float32)
    centred = rows - jnp.mean(rows, axis=1, keepdims=True)
    spread = jnp.mean(centred * centred, axis=1, keepdims=True)
    normed = (centred * lax.rsqrt(spread + 1e-5) * gain_ref[...]).astype(jnp.bfloat16)
    left = dot_t(normed, weight_ref[0])
    right = dot_t(normed, weight_ref[1])
    frame = pl.program_id(0) * rows.shape[0] + lax.broadcasted_iota(jnp.int32, (rows.shape[0], 1), 0)
    gated = left * (1.0 / (1.0 + jnp.exp(-right)))
    gated_ref[...] = jnp.where(frame < count_ref[0], gated, 0.0).astype(gated_ref.dtype)
    pooled_ref[...] = jnp.dot(pooling(rows.shape[0]), audio, preferred_element_type=jnp.float32)


def gate(left_frames, audio, gain, weight):
    frames, width = audio.shape
    columns = weight.shape[1]
    block = 256
    return pl.pallas_call(
        gate_kernel,
        grid=(frames // block,),
        in_specs=[
            pl.BlockSpec(memory_space=pltpu.SMEM),
            pl.BlockSpec((block, width), lambda i: (i, 0)),
            pl.BlockSpec((1, width), lambda i: (0, 0)),
            pl.BlockSpec((2, columns, width), lambda i: (0, 0, 0)),
        ],
        out_specs=[
            pl.BlockSpec((block, columns), lambda i: (i, 0)),
            pl.BlockSpec((block // 4, width), lambda i: (i, 0)),
        ],
        out_shape=[
            jax.ShapeDtypeStruct((frames, columns), jnp.bfloat16),
            jax.ShapeDtypeStruct((frames // 4, width), jnp.float32),
        ],
        compiler_params=pltpu.CompilerParams(vmem_limit_bytes=20 * MIB),
        cost_estimate=pl.CostEstimate(
            flops=4 * frames * width * columns, bytes_accessed=2 * frames * width * 4, transcendentals=frames * columns
        ),
        name="gate",
    )(left_frames, audio, gain, weight)


EDGE = 16


def conv_kernel(before_ref, gated_ref, after_ref, taps_ref, pw_ref, *refs):
    term_ref, padded, act = refs[-3:]
    frames, columns = gated_ref.shape
    taps = taps_ref.shape[0]
    padded[:EDGE] = before_ref[...].astype(jnp.float32)
    padded[EDGE : EDGE + frames] = gated_ref[...].astype(jnp.float32)
    padded[EDGE + frames :] = after_ref[...].astype(jnp.float32)
    chunk = 64
    lead = EDGE - (taps - 1) // 2
    for at in range(0, columns, 128):
        lanes = slice(at, min(at + 128, columns))

        def body(i, carry, lanes=lanes):
            first = pl.multiple_of(i * chunk, chunk)
            window = padded[pl.ds(first, chunk + 2 * EDGE), lanes]
            total = jnp.zeros((chunk, window.shape[1]), jnp.float32)
            for turn in range(8):
                turned_by = window if turn == 0 else pltpu.roll(window, window.shape[0] - turn, 0)
                for offset in range(turn, lead + taps, 8):
                    if offset >= lead:
                        start = offset - turn
                        total = total + turned_by[start : start + chunk] * taps_ref[offset - lead, lanes][None]
            value = total * (1.0 / (1.0 + jnp.exp(-total)))
            act[pl.ds(first, chunk), lanes] = value.astype(jnp.bfloat16)
            return carry

        lax.fori_loop(0, frames // chunk, body, 0)
    pooled = jnp.dot(pooling(frames), act[...], preferred_element_type=jnp.float32).astype(jnp.bfloat16)
    term_ref[...] = jnp.dot(pooled, pw_ref[...], preferred_element_type=jnp.float32).astype(term_ref.dtype)


def conv(before, gated, after, taps, pw, *after_these):
    frames, columns = gated.shape
    vmem = pl.BlockSpec(memory_space=pltpu.VMEM)
    return pl.pallas_call(
        conv_kernel,
        in_specs=[vmem] * 5 + [pl.BlockSpec(memory_space=pl.ANY)] * len(after_these),
        out_specs=vmem,
        out_shape=jax.ShapeDtypeStruct((frames // 4, pw.shape[1]), jnp.bfloat16),
        scratch_shapes=[
            pltpu.VMEM((frames + 2 * EDGE, columns), jnp.float32),
            pltpu.VMEM((frames, columns), jnp.bfloat16),
        ],
        compiler_params=pltpu.CompilerParams(vmem_limit_bytes=12 * MIB),
        cost_estimate=pl.CostEstimate(
            flops=5_000_000_000, bytes_accessed=2 * frames * columns * 4, transcendentals=frames * columns
        ),
        name="conv",
    )(before, gated, after, taps, pw, *after_these)


def add_kernel(tag_ref, a_ref, b_ref, total_ref, sent_ref, same_ref):
    same_ref[0] = tag_ref[0]
    total = a_ref[...].astype(jnp.float32) + b_ref[...].astype(jnp.float32)
    total_ref[...] = total
    sent_ref[...] = total.astype(sent_ref.dtype)


def add(tag, a, b):
    vmem, smem = pl.BlockSpec(memory_space=pltpu.VMEM), pl.BlockSpec(memory_space=pltpu.SMEM)
    return pl.pallas_call(
        add_kernel,
        in_specs=[smem, vmem, vmem],
        out_specs=[vmem, vmem, smem],
        out_shape=[
            jax.ShapeDtypeStruct(a.shape, jnp.float32),
            jax.ShapeDtypeStruct(a.shape, jnp.bfloat16),
            jax.ShapeDtypeStruct((1,), jnp.int32),
        ],
        compiler_params=pltpu.CompilerParams(vmem_limit_bytes=8 * MIB),
        name="add",
    )(tag, a, b)


def place(shift_x, shift_y):
    return [
        ((x * NY + y) * 2 + c, ((x + shift_x) % NX * NY + (y + shift_y) % NY) * 2 + c)
        for x in range(NX)
        for y in range(NY)
        for c in range(2)
    ]


SWAP = [(i, i ^ 1) for i in range(NX * NY * 2)]


def of_group(group, pairs):
    count = NX * NY * 2
    return [(group * count + i, group * count + j) for i, j in pairs]


def spread(block):
    send = lambda v, dx, dy: lax.ppermute(v, ("grp", "seq"), of_group(0, place(dx, dy)))
    rows = block.shape[0]
    near = jnp.concatenate([send(block, 0, 1), block, send(block, 0, -1)], axis=0)
    line = jnp.concatenate([near, send(near, 0, -3), send(near[rows:], 0, 3)], axis=0)
    steps = [-1, 0, 1, 2, 3, 4, -3, -2]
    return [(0, steps, line)] + [(dx, steps, send(line, -dx, 0)) for dx in (-1, 1, 2)]


def pooled_kernel(audio_ref, term_ref, other_ref, expand_ref, out_ref):
    pooled = (audio_ref[...] + term_ref[...] + other_ref[...].astype(jnp.float32)).astype(jnp.bfloat16)
    out_ref[...] = jnp.dot(pooled, expand_ref[...], preferred_element_type=jnp.float32).astype(jnp.bfloat16)


def pooled_part(pooled_audio, term, other, expand):
    vmem = pl.BlockSpec(memory_space=pltpu.VMEM)
    return pl.pallas_call(
        pooled_kernel,
        in_specs=[vmem] * 4,
        out_specs=vmem,
        out_shape=jax.ShapeDtypeStruct((pooled_audio.shape[0], expand.shape[1]), jnp.bfloat16),
        compiler_params=pltpu.CompilerParams(vmem_limit_bytes=12 * MIB),
        cost_estimate=pl.CostEstimate(flops=5_000_000_000, bytes_accessed=8000000, transcendentals=0),
        name="pooled_part",
    )(pooled_audio, term, other, expand)


def tokens_kernel(*refs, counts):
    pieces = refs[: len(counts)]
    pooled_ref = refs[len(counts)]
    out_ref, weight, sem = refs[-3:]
    copies = []
    at = 0
    for i, (ref, count) in enumerate(zip(pieces, counts, strict=True)):
        copies.append(pltpu.make_async_copy(ref, weight.at[at : at + count], sem.at[i]))
        at += count
    for copy in copies:
        copy.start()
    for copy in copies:
        copy.wait()
    out_ref[...] = jnp.dot(pooled_ref[...], weight[...], preferred_element_type=jnp.float32).astype(out_ref.dtype)


def tokens_part(pieces, pooled, *after_these):
    counts = [p.shape[0] for p in pieces]
    count = pooled.shape[0]
    columns = pieces[0].shape[1]
    anywhere = pl.BlockSpec(memory_space=pl.ANY)
    vmem = pl.BlockSpec(memory_space=pltpu.VMEM)
    return pl.pallas_call(
        functools.partial(tokens_kernel, counts=counts),
        in_specs=[anywhere] * len(pieces) + [vmem] + [anywhere] * len(after_these),
        out_specs=vmem,
        out_shape=jax.ShapeDtypeStruct((count, columns), jnp.bfloat16),
        scratch_shapes=[
            pltpu.VMEM((sum(counts), columns), jnp.bfloat16),
            pltpu.SemaphoreType.DMA((len(pieces),)),
        ],
        compiler_params=pltpu.CompilerParams(vmem_limit_bytes=60 * MIB),
        cost_estimate=pl.CostEstimate(
            flops=4 * count * sum(counts) * columns, bytes_accessed=8000000, transcendentals=0
        ),
        name="tokens_part",
    )(*pieces, pooled, *after_these)


def shards(
    audio, frame_count, ln_gain, glu_weight, dw_kernel, pw_weight, adapt_weight, text, norm_gain, qkv_weight, qkv_bias
):
    grp = lax.axis_index("grp")
    mdl = lax.axis_index("mdl")
    seq = lax.axis_index("seq")
    core, y, x = seq % 2, seq // 2 % NY, seq // (2 * NY)
    n_mdl = lax.axis_size("mdl")
    both = ("grp", "mdl")
    rows, width = adapt_weight.shape
    ring = lambda group, k: [(group * n_mdl + i, group * n_mdl + (i + k) % n_mdl) for i in range(n_mdl)]

    weight = lax.all_gather(qkv_weight, "seq", axis=0, tiled=True)
    pieces = spread(adapt_weight)
    swap = lambda v: lax.ppermute(v, ("grp", "seq"), of_group(0, SWAP))
    adapter = [p for _, _, p in pieces]
    adapter += [swap(adapter[0])]

    behind = lax.ppermute(text, both, ring(1, 1))
    ahead = lax.ppermute(text, both, ring(1, -1))
    second = lax.ppermute(behind, both, ring(1, 1))
    words = [text, ahead, second, behind]

    frames = audio.shape[0]
    gated, pooled_audio = gate(
        frame_count - seq * frames, audio, ln_gain[None], jnp.swapaxes(glu_weight, 1, 2)
    )
    up = [(i, i + 1) for i in range(lax.axis_size("seq") - 1)]
    before_edge = lax.ppermute(gated[frames - EDGE :], ("grp", "seq"), of_group(0, up))
    after_edge = lax.ppermute(gated[:EDGE], ("grp", "seq"), of_group(0, [(j, i) for i, j in up]))
    term = conv(before_edge, gated, after_edge, dw_kernel, pw_weight, behind, ahead)
    neighbour = lax.ppermute(term, both, [(0, 1), (1, 0), (2, 3), (3, 2)])
    term, rounded, tag = add(core[None], term, neighbour)
    other = lax.ppermute(rounded, both, [(1, 2), (2, 1), (3, 0), (0, 3)])
    adapter += [swap(jnp.where(tag[0] >= 0, jnp.concatenate(adapter[1:4], axis=0), 0))]

    chips = jnp.concatenate(
        [
            jnp.stack([(x + dx) % NX * NY + (y + dy) % NY for dy in steps])
            for dx, steps, _ in pieces
        ]
    )
    device = jnp.concatenate([2 * chips + core, 2 * chips + 1 - core])
    source = (device[:, None] * rows + jnp.arange(rows, dtype=jnp.int32)[None]).reshape(-1)
    expand = (jnp.arange(audio.shape[1], dtype=jnp.int32)[:, None] == source[None]).astype(jnp.bfloat16)
    tokens = tokens_part(adapter, pooled_part(pooled_audio, term, other, expand), second)

    tables = rotary_tables(2 * text.shape[0])
    gain = norm_gain.reshape(n_mdl, 1, width)
    order = (mdl + jnp.arange(n_mdl, dtype=jnp.int32)) % n_mdl
    order_of = (2, -1, 0, 1)
    sent = {
        k: lax.ppermute(tokens, both, [(i, n_mdl + (i + k) % n_mdl) for i in range(n_mdl)]) for k in order_of
    }
    sounds = [sent[0], sent[-1], sent[2], sent[1]]
    context = decode(order, words, sounds, gain, weight, qkv_bias[None], tables)
    return jnp.where(grp == 0, tokens, context)[None]


def solution(mesh):
    in_specs = (
        P("seq", None),
        P(),
        P(),
        P(None, None, "mdl"),
        P(None, "mdl"),
        P("mdl", None),
        P("seq", "mdl"),
        P("seq", "mdl"),
        P(),
        P("seq", "mdl"),
        P("mdl"),
    )
    out_specs = P("grp", "seq", "mdl")
    return jax.shard_map(shards, mesh=mesh, in_specs=in_specs, out_specs=out_specs, check_vma=False)
```

```python
import functools

import jax
import jax.numpy as jnp
from jax import lax
from jax.experimental import pallas as pl
from jax.experimental.pallas import tpu as pltpu
from jax.sharding import PartitionSpec as P

HEADS = 28
KV = 4
HEAD = 128
MIB = 1024 * 1024
LOG2E = 1.4426950408889634
NX = 4
NY = 8


def rotary_tables(count):
    half = HEAD // 2
    freq = 1000000.0 ** (-(jnp.arange(half, dtype=jnp.float32) * 2.0 / HEAD))
    angle = jnp.arange(count, dtype=jnp.int32).astype(jnp.float32)[:, None] * freq[None, :]
    cosine, sine = jnp.cos(angle), jnp.sin(angle)
    return jnp.concatenate([cosine, cosine], 1), jnp.concatenate([-sine, sine], 1)


def turned(values, cosine, sine):
    return values * cosine + pltpu.roll(values, HEAD // 2, 1) * sine


def decode_kernel(
    order_ref, *refs, parts
):
    ins = refs[: 2 * parts]
    gain_ref, w_ref, bias_ref, cos_ref, sin_ref, out_ref, held, rows, scales, acc, acc_kv, sem = refs[2 * parts :]
    step = pl.program_id(0)
    count, total = acc.shape
    heads = total // HEAD - 2
    width = held.shape[2]

    @pl.when(step == 0)
    def _():
        copies = [pltpu.make_async_copy(ref, held.at[i], sem.at[i]) for i, ref in enumerate(ins)]
        for copy in copies:
            copy.start()
        for first, side in ((0, 0), (count, parts)):
            square = jnp.zeros((count, 1), jnp.float32)
            for i in range(parts):
                copies[side + i].wait()
                block = order_ref[i]
                x = held[side + i].astype(jnp.float32)
                square = square + jnp.sum(x * x, axis=1, keepdims=True)
                rows[block, first : first + count] = (x * gain_ref[block]).astype(jnp.bfloat16)
            scales[first : first + count] = lax.rsqrt(square / (parts * width) + 1e-6)

    text = jnp.dot(rows[step, :count], w_ref[...], preferred_element_type=jnp.float32)
    audio = jnp.dot(rows[step, count:], w_ref[:, heads * HEAD :], preferred_element_type=jnp.float32)

    @pl.when(step == 0)
    def _():
        acc[...] = text
        acc_kv[...] = audio

    @pl.when(step > 0)
    def _():
        acc[...] += text
        acc_kv[...] += audio

    @pl.when(step == pl.num_programs(0) - 1)
    def _():
        scale, scale_kv = scales[:count], scales[count:]
        cosine, sine = cos_ref[count:], sin_ref[count:]
        key_cols = slice(heads * HEAD, (heads + 1) * HEAD)
        value_cols = slice((heads + 1) * HEAD, total)
        keys = jnp.concatenate(
            [
                turned(acc_kv[:, :HEAD] * scale_kv + bias_ref[:, key_cols], cos_ref[:count], sin_ref[:count]),
                turned(acc[:, key_cols] * scale + bias_ref[:, key_cols], cosine, sine),
            ],
            axis=0,
        ).astype(jnp.bfloat16)
        values = jnp.concatenate(
            [
                acc_kv[:, HEAD:] * scale_kv + bias_ref[:, value_cols],
                acc[:, value_cols] * scale + bias_ref[:, value_cols],
            ],
            axis=0,
        ).astype(jnp.bfloat16)
        row = lax.broadcasted_iota(jnp.int32, (count, 2 * count), 0)
        col = lax.broadcasted_iota(jnp.int32, (count, 2 * count), 1)
        allowed = col <= row + count
        for h in range(heads):
            cols = slice(h * HEAD, (h + 1) * HEAD)
            query = turned(acc[:, cols] * scale + bias_ref[:, cols], cosine, sine) * (LOG2E * HEAD**-0.5)
            scores = dot_t(query.astype(jnp.bfloat16), keys)
            scores = jnp.where(allowed, scores, -1e30)
            weights = jnp.exp2(scores - jnp.max(scores, axis=1, keepdims=True))
            probs = weights * (1.0 / jnp.sum(weights, axis=1, keepdims=True))
            out_ref[:, cols] = jnp.dot(
                probs.astype(jnp.bfloat16), values, preferred_element_type=jnp.float32
            ).astype(jnp.bfloat16)


def decode(order, words, sounds, gain, weight, bias, tables):
    parts = len(words)
    count, width = words[0].shape
    total = weight.shape[1]
    columns = total - 2 * HEAD
    whole = lambda *shape: pl.BlockSpec(shape, lambda k: (0,) * len(shape))
    return pl.pallas_call(
        functools.partial(decode_kernel, parts=parts),
        grid=(parts,),
        in_specs=[pl.BlockSpec(memory_space=pltpu.SMEM)]
        + [pl.BlockSpec(memory_space=pl.ANY)] * (2 * parts)
        + [
            whole(parts, 1, width),
            pl.BlockSpec((width, total), lambda k: (k, 0)),
            whole(1, total),
            whole(2 * count, HEAD),
            whole(2 * count, HEAD),
        ],
        out_specs=whole(count, columns),
        scratch_shapes=[
            pltpu.VMEM((2 * parts, count, width), jnp.bfloat16),
            pltpu.VMEM((parts, 2 * count, width), jnp.bfloat16),
            pltpu.VMEM((2 * count, 1), jnp.float32),
            pltpu.VMEM((count, total), jnp.float32),
            pltpu.VMEM((count, 2 * HEAD), jnp.float32),
            pltpu.SemaphoreType.DMA((2 * parts,)),
        ],
        out_shape=jax.ShapeDtypeStruct((count, columns), jnp.bfloat16),
        compiler_params=pltpu.CompilerParams(vmem_limit_bytes=56 * MIB),
        cost_estimate=pl.CostEstimate(
            flops=2 * count * parts * width * total, bytes_accessed=2 * parts * width * (total + count), transcendentals=0
        ),
        name="decode",
    )(order, *words, *sounds, gain, weight, bias, *tables)


def pooling(rows):
    r = lax.broadcasted_iota(jnp.int32, (rows // 4, rows), 0)
    c = lax.broadcasted_iota(jnp.int32, (rows // 4, rows), 1)
    return jnp.where((c >= 4 * r) & (c < 4 * r + 4), 0.25, 0.0).astype(jnp.bfloat16)


def dot_t(a, b):
    return lax.dot_general(a, b, (((1,), (1,)), ((), ())), preferred_element_type=jnp.float32)


def gate_kernel(count_ref, audio_ref, gain_ref, weight_ref, gated_ref, pooled_ref):
    audio = audio_ref[...]
    rows = audio.astype(jnp.float32)
    centred = rows - jnp.mean(rows, axis=1, keepdims=True)
    spread = jnp.mean(centred * centred, axis=1, keepdims=True)
    normed = (centred * lax.rsqrt(spread + 1e-5) * gain_ref[...]).astype(jnp.bfloat16)
    left = dot_t(normed, weight_ref[0])
    right = dot_t(normed, weight_ref[1])
    frame = pl.program_id(0) * rows.shape[0] + lax.broadcasted_iota(jnp.int32, (rows.shape[0], 1), 0)
    gated = left * (1.0 / (1.0 + jnp.exp(-right)))
    gated_ref[...] = jnp.where(frame < count_ref[0], gated, 0.0).astype(gated_ref.dtype)
    pooled_ref[...] = jnp.dot(pooling(rows.shape[0]), audio, preferred_element_type=jnp.float32)


def gate(left_frames, audio, gain, weight):
    frames, width = audio.shape
    columns = weight.shape[1]
    block = 256
    return pl.pallas_call(
        gate_kernel,
        grid=(frames // block,),
        in_specs=[
            pl.BlockSpec(memory_space=pltpu.SMEM),
            pl.BlockSpec((block, width), lambda i: (i, 0)),
            pl.BlockSpec((1, width), lambda i: (0, 0)),
            pl.BlockSpec((2, columns, width), lambda i: (0, 0, 0)),
        ],
        out_specs=[
            pl.BlockSpec((block, columns), lambda i: (i, 0)),
            pl.BlockSpec((block // 4, width), lambda i: (i, 0)),
        ],
        out_shape=[
            jax.ShapeDtypeStruct((frames, columns), jnp.bfloat16),
            jax.ShapeDtypeStruct((frames // 4, width), jnp.float32),
        ],
        compiler_params=pltpu.CompilerParams(vmem_limit_bytes=20 * MIB),
        cost_estimate=pl.CostEstimate(
            flops=4 * frames * width * columns, bytes_accessed=2 * frames * width * 4, transcendentals=frames * columns
        ),
        name="gate",
    )(left_frames, audio, gain, weight)


EDGE = 16


def conv_kernel(before_ref, gated_ref, after_ref, taps_ref, pw_ref, *refs):
    term_ref, padded, act = refs[-3:]
    frames, columns = gated_ref.shape
    taps = taps_ref.shape[0]
    padded[:EDGE] = before_ref[...].astype(jnp.float32)
    padded[EDGE : EDGE + frames] = gated_ref[...].astype(jnp.float32)
    padded[EDGE + frames :] = after_ref[...].astype(jnp.float32)
    chunk = 64
    lead = EDGE - (taps - 1) // 2
    for at in range(0, columns, 128):
        lanes = slice(at, min(at + 128, columns))

        def body(i, carry, lanes=lanes):
            first = pl.multiple_of(i * chunk, chunk)
            window = padded[pl.ds(first, chunk + 2 * EDGE), lanes]
            total = jnp.zeros((chunk, window.shape[1]), jnp.float32)
            for turn in range(8):
                turned_by = window if turn == 0 else pltpu.roll(window, window.shape[0] - turn, 0)
                for offset in range(turn, lead + taps, 8):
                    if offset >= lead:
                        start = offset - turn
                        total = total + turned_by[start : start + chunk] * taps_ref[offset - lead, lanes][None]
            value = total * (1.0 / (1.0 + jnp.exp(-total)))
            act[pl.ds(first, chunk), lanes] = value.astype(jnp.bfloat16)
            return carry

        lax.fori_loop(0, frames // chunk, body, 0)
    pooled = jnp.dot(pooling(frames), act[...], preferred_element_type=jnp.float32).astype(jnp.bfloat16)
    term_ref[...] = jnp.dot(pooled, pw_ref[...], preferred_element_type=jnp.float32).astype(term_ref.dtype)


def conv(before, gated, after, taps, pw, *after_these):
    frames, columns = gated.shape
    vmem = pl.BlockSpec(memory_space=pltpu.VMEM)
    return pl.pallas_call(
        conv_kernel,
        in_specs=[vmem] * 5 + [pl.BlockSpec(memory_space=pl.ANY)] * len(after_these),
        out_specs=vmem,
        out_shape=jax.ShapeDtypeStruct((frames // 4, pw.shape[1]), jnp.bfloat16),
        scratch_shapes=[
            pltpu.VMEM((frames + 2 * EDGE, columns), jnp.float32),
            pltpu.VMEM((frames, columns), jnp.bfloat16),
        ],
        compiler_params=pltpu.CompilerParams(vmem_limit_bytes=12 * MIB),
        cost_estimate=pl.CostEstimate(
            flops=5_000_000_000, bytes_accessed=2 * frames * columns * 4, transcendentals=frames * columns
        ),
        name="conv",
    )(before, gated, after, taps, pw, *after_these)


def place(shift_x, shift_y):
    return [
        ((x * NY + y) * 2 + c, ((x + shift_x) % NX * NY + (y + shift_y) % NY) * 2 + c)
        for x in range(NX)
        for y in range(NY)
        for c in range(2)
    ]


SWAP = [(i, i ^ 1) for i in range(NX * NY * 2)]


def of_group(group, pairs):
    count = NX * NY * 2
    return [(group * count + i, group * count + j) for i, j in pairs]


def spread(block):
    send = lambda v, dx, dy: lax.ppermute(v, ("grp", "seq"), of_group(0, place(dx, dy)))
    rows = block.shape[0]
    near = jnp.concatenate([send(block, 0, 1), block, send(block, 0, -1)], axis=0)
    line = jnp.concatenate([near, send(near, 0, -3), send(near[rows:], 0, 3)], axis=0)
    steps = [-1, 0, 1, 2, 3, 4, -3, -2]
    return [(0, steps, line)] + [(dx, steps, send(line, -dx, 0)) for dx in (-1, 1, 2)]


def tokens_kernel(*refs, counts):
    pieces = refs[: len(counts)]
    audio_ref, term_ref, other_ref, expand_ref = refs[len(counts) : len(counts) + 4]
    out_ref, weight = refs[-2:]
    at = 0
    for ref, count in zip(pieces, counts, strict=True):
        weight[at : at + count] = ref[...]
        at += count
    pooled = (audio_ref[...] + term_ref[...] + other_ref[...].astype(jnp.float32)).astype(jnp.bfloat16)
    ordered = jnp.dot(pooled, expand_ref[...], preferred_element_type=jnp.float32).astype(jnp.bfloat16)
    out_ref[...] = jnp.dot(ordered, weight[...], preferred_element_type=jnp.float32).astype(out_ref.dtype)


def tokens_part(pieces, pooled_audio, term, other, expand, *after_these):
    counts = [p.shape[0] for p in pieces]
    count = pooled_audio.shape[0]
    columns = pieces[0].shape[1]
    vmem = pl.BlockSpec(memory_space=pltpu.VMEM)
    return pl.pallas_call(
        functools.partial(tokens_kernel, counts=counts),
        in_specs=[vmem] * (len(pieces) + 4) + [pl.BlockSpec(memory_space=pl.ANY)] * len(after_these),
        out_specs=vmem,
        out_shape=jax.ShapeDtypeStruct((count, columns), jnp.bfloat16),
        scratch_shapes=[pltpu.VMEM((sum(counts), columns), jnp.bfloat16)],
        compiler_params=pltpu.CompilerParams(vmem_limit_bytes=20 * MIB),
        cost_estimate=pl.CostEstimate(
            flops=4 * count * sum(counts) * columns, bytes_accessed=8000000, transcendentals=0
        ),
        name="tokens_part",
    )(*pieces, pooled_audio, term, other, expand, *after_these)


def shards(
    audio, frame_count, ln_gain, glu_weight, dw_kernel, pw_weight, adapt_weight, text, norm_gain, qkv_weight, qkv_bias
):
    grp = lax.axis_index("grp")
    mdl = lax.axis_index("mdl")
    seq = lax.axis_index("seq")
    core, y, x = seq % 2, seq // 2 % NY, seq // (2 * NY)
    n_mdl = lax.axis_size("mdl")
    both = ("grp", "mdl")
    rows, width = adapt_weight.shape
    ring = lambda group, k: [(group * n_mdl + i, group * n_mdl + (i + k) % n_mdl) for i in range(n_mdl)]

    weight = lax.all_gather(qkv_weight, "seq", axis=0, tiled=True)
    pieces = spread(adapt_weight)
    swap = lambda v: lax.ppermute(v, ("grp", "seq"), of_group(0, SWAP))
    adapter = [p for _, _, p in pieces]
    adapter += [swap(adapter[0]), swap(jnp.concatenate(adapter[1:], axis=0))]

    behind = lax.ppermute(text, both, ring(1, 1))
    ahead = lax.ppermute(text, both, ring(1, -1))
    second = lax.ppermute(behind, both, ring(1, 1))
    words = [text, ahead, second, behind]

    frames = audio.shape[0]
    gated, pooled_audio = gate(
        frame_count - seq * frames, audio, ln_gain[None], jnp.swapaxes(glu_weight, 1, 2)
    )
    up = [(i, i + 1) for i in range(lax.axis_size("seq") - 1)]
    before_edge = lax.ppermute(gated[frames - EDGE :], ("grp", "seq"), of_group(0, up))
    after_edge = lax.ppermute(gated[:EDGE], ("grp", "seq"), of_group(0, [(j, i) for i, j in up]))
    term = conv(before_edge, gated, after_edge, dw_kernel, pw_weight, behind, ahead)
    term = term.astype(jnp.float32) + lax.ppermute(
        term, both, [(0, 1), (1, 0), (2, 3), (3, 2)]
    ).astype(jnp.float32)
    other = lax.ppermute(term.astype(jnp.bfloat16), both, [(1, 2), (2, 1), (3, 0), (0, 3)])

    chips = jnp.concatenate(
        [
            jnp.stack([(x + dx) % NX * NY + (y + dy) % NY for dy in steps])
            for dx, steps, _ in pieces
        ]
    )
    device = jnp.concatenate([2 * chips + core, 2 * chips + 1 - core])
    source = (device[:, None] * rows + jnp.arange(rows, dtype=jnp.int32)[None]).reshape(-1)
    expand = (jnp.arange(audio.shape[1], dtype=jnp.int32)[:, None] == source[None]).astype(jnp.bfloat16)
    tokens = tokens_part(adapter, pooled_audio, term, other, expand, second)

    tables = rotary_tables(2 * text.shape[0])
    gain = norm_gain.reshape(n_mdl, 1, width)
    order = (mdl + jnp.arange(n_mdl, dtype=jnp.int32)) % n_mdl
    same = lax.ppermute(tokens, both, [(i, n_mdl + i) for i in range(n_mdl)])
    following = lax.ppermute(tokens, both, [(i, n_mdl + (i - 1) % n_mdl) for i in range(n_mdl)])
    across = lax.ppermute(following, both, ring(1, -1))
    last = lax.ppermute(same, both, ring(1, 1))
    sounds = [same, following, across, last]
    context = decode(order, words, sounds, gain, weight, qkv_bias[None], tables)
    return jnp.where(grp == 0, tokens, context)[None]


def solution(mesh):
    in_specs = (
        P("seq", None),
        P(),
        P(),
        P(None, None, "mdl"),
        P(None, "mdl"),
        P("mdl", None),
        P("seq", "mdl"),
        P("seq", "mdl"),
        P(),
        P("seq", "mdl"),
        P("mdl"),
    )
    out_specs = P("grp", "seq", "mdl")
    return jax.shard_map(shards, mesh=mesh, in_specs=in_specs, out_specs=out_specs, check_vma=False)
```

```python
import functools

import jax
import jax.numpy as jnp
from jax import lax
from jax.experimental import pallas as pl
from jax.experimental.pallas import tpu as pltpu
from jax.sharding import PartitionSpec as P

HEADS = 28
KV = 4
HEAD = 128
MIB = 1024 * 1024
LOG2E = 1.4426950408889634
NX = 4
NY = 8


def rotary_tables(count):
    half = HEAD // 2
    freq = 1000000.0 ** (-(jnp.arange(half, dtype=jnp.float32) * 2.0 / HEAD))
    angle = jnp.arange(count, dtype=jnp.int32).astype(jnp.float32)[:, None] * freq[None, :]
    cosine, sine = jnp.cos(angle), jnp.sin(angle)
    return jnp.concatenate([cosine, cosine], 1), jnp.concatenate([-sine, sine], 1)


def turned(values, cosine, sine):
    return values * cosine + pltpu.roll(values, HEAD // 2, 1) * sine


def decode_kernel(
    order_ref, *refs, parts
):
    ins = refs[: 2 * parts]
    gain_ref, w_ref, bias_ref, cos_ref, sin_ref, out_ref, held, rows, scales, acc, acc_kv, sem = refs[2 * parts :]
    step = pl.program_id(0)
    count, total = acc.shape
    heads = total // HEAD - 2
    width = held.shape[2]

    @pl.when(step == 0)
    def _():
        copies = [pltpu.make_async_copy(ref, held.at[i], sem.at[i]) for i, ref in enumerate(ins)]
        for copy in copies:
            copy.start()
        for first, side in ((0, 0), (count, parts)):
            square = jnp.zeros((count, 1), jnp.float32)
            for i in range(parts):
                copies[side + i].wait()
                block = order_ref[i]
                x = held[side + i].astype(jnp.float32)
                square = square + jnp.sum(x * x, axis=1, keepdims=True)
                rows[block, first : first + count] = (x * gain_ref[block]).astype(jnp.bfloat16)
            scales[first : first + count] = lax.rsqrt(square / (parts * width) + 1e-6)

    text = jnp.dot(rows[step, :count], w_ref[...], preferred_element_type=jnp.float32)
    audio = jnp.dot(rows[step, count:], w_ref[:, heads * HEAD :], preferred_element_type=jnp.float32)

    @pl.when(step == 0)
    def _():
        acc[...] = text
        acc_kv[...] = audio

    @pl.when(step > 0)
    def _():
        acc[...] += text
        acc_kv[...] += audio

    @pl.when(step == pl.num_programs(0) - 1)
    def _():
        scale, scale_kv = scales[:count], scales[count:]
        cosine, sine = cos_ref[count:], sin_ref[count:]
        key_cols = slice(heads * HEAD, (heads + 1) * HEAD)
        value_cols = slice((heads + 1) * HEAD, total)
        keys = jnp.concatenate(
            [
                turned(acc_kv[:, :HEAD] * scale_kv + bias_ref[:, key_cols], cos_ref[:count], sin_ref[:count]),
                turned(acc[:, key_cols] * scale + bias_ref[:, key_cols], cosine, sine),
            ],
            axis=0,
        ).astype(jnp.bfloat16)
        values = jnp.concatenate(
            [
                acc_kv[:, HEAD:] * scale_kv + bias_ref[:, value_cols],
                acc[:, value_cols] * scale + bias_ref[:, value_cols],
            ],
            axis=0,
        ).astype(jnp.bfloat16)
        values = jnp.concatenate([values, jnp.ones_like(values)], axis=1)
        row = lax.broadcasted_iota(jnp.int32, (count, 2 * count), 0)
        col = lax.broadcasted_iota(jnp.int32, (count, 2 * count), 1)
        allowed = col <= row + count
        for h in range(heads):
            cols = slice(h * HEAD, (h + 1) * HEAD)
            query = turned(acc[:, cols] * scale + bias_ref[:, cols], cosine, sine) * (LOG2E * HEAD**-0.5)
            scores = dot_t(query.astype(jnp.bfloat16), keys)
            scores = jnp.where(allowed, scores, -1e30)
            weights = jnp.exp2(scores - jnp.max(scores, axis=1, keepdims=True))
            context = jnp.dot(weights.astype(jnp.bfloat16), values, preferred_element_type=jnp.float32)
            out_ref[:, cols] = (context[:, :HEAD] * (1.0 / context[:, HEAD:])).astype(jnp.bfloat16)


def decode(order, words, sounds, gain, weight, bias, tables):
    parts = len(words)
    count, width = words[0].shape
    total = weight.shape[1]
    columns = total - 2 * HEAD
    whole = lambda *shape: pl.BlockSpec(shape, lambda k: (0,) * len(shape))
    return pl.pallas_call(
        functools.partial(decode_kernel, parts=parts),
        grid=(parts,),
        in_specs=[pl.BlockSpec(memory_space=pltpu.SMEM)]
        + [pl.BlockSpec(memory_space=pl.ANY)] * (2 * parts)
        + [
            whole(parts, 1, width),
            pl.BlockSpec((width, total), lambda k: (k, 0)),
            whole(1, total),
            whole(2 * count, HEAD),
            whole(2 * count, HEAD),
        ],
        out_specs=whole(count, columns),
        scratch_shapes=[
            pltpu.VMEM((2 * parts, count, width), jnp.bfloat16),
            pltpu.VMEM((parts, 2 * count, width), jnp.bfloat16),
            pltpu.VMEM((2 * count, 1), jnp.float32),
            pltpu.VMEM((count, total), jnp.float32),
            pltpu.VMEM((count, 2 * HEAD), jnp.float32),
            pltpu.SemaphoreType.DMA((2 * parts,)),
        ],
        out_shape=jax.ShapeDtypeStruct((count, columns), jnp.bfloat16),
        compiler_params=pltpu.CompilerParams(vmem_limit_bytes=56 * MIB),
        cost_estimate=pl.CostEstimate(
            flops=2 * count * parts * width * total, bytes_accessed=2 * parts * width * (total + count), transcendentals=0
        ),
        name="decode",
    )(order, *words, *sounds, gain, weight, bias, *tables)


def pooling(rows):
    r = lax.broadcasted_iota(jnp.int32, (rows // 4, rows), 0)
    c = lax.broadcasted_iota(jnp.int32, (rows // 4, rows), 1)
    return jnp.where((c >= 4 * r) & (c < 4 * r + 4), 0.25, 0.0).astype(jnp.bfloat16)


def dot_t(a, b):
    return lax.dot_general(a, b, (((1,), (1,)), ((), ())), preferred_element_type=jnp.float32)


def gate_kernel(count_ref, audio_ref, gain_ref, weight_ref, gated_ref, pooled_ref):
    audio = audio_ref[...]
    rows = audio.astype(jnp.float32)
    centred = rows - jnp.mean(rows, axis=1, keepdims=True)
    spread = jnp.mean(centred * centred, axis=1, keepdims=True)
    normed = (centred * lax.rsqrt(spread + 1e-5) * gain_ref[...]).astype(jnp.bfloat16)
    left = dot_t(normed, weight_ref[0])
    right = dot_t(normed, weight_ref[1])
    frame = pl.program_id(0) * rows.shape[0] + lax.broadcasted_iota(jnp.int32, (rows.shape[0], 1), 0)
    gated = left * (1.0 / (1.0 + jnp.exp(-right)))
    gated_ref[...] = jnp.where(frame < count_ref[0], gated, 0.0).astype(gated_ref.dtype)
    pooled_ref[...] = jnp.dot(pooling(rows.shape[0]), audio, preferred_element_type=jnp.float32)


def gate(left_frames, audio, gain, weight):
    frames, width = audio.shape
    columns = weight.shape[1]
    block = 256
    return pl.pallas_call(
        gate_kernel,
        grid=(frames // block,),
        in_specs=[
            pl.BlockSpec(memory_space=pltpu.SMEM),
            pl.BlockSpec((block, width), lambda i: (i, 0)),
            pl.BlockSpec((1, width), lambda i: (0, 0)),
            pl.BlockSpec((2, columns, width), lambda i: (0, 0, 0)),
        ],
        out_specs=[
            pl.BlockSpec((block, columns), lambda i: (i, 0)),
            pl.BlockSpec((block // 4, width), lambda i: (i, 0)),
        ],
        out_shape=[
            jax.ShapeDtypeStruct((frames, columns), jnp.bfloat16),
            jax.ShapeDtypeStruct((frames // 4, width), jnp.float32),
        ],
        compiler_params=pltpu.CompilerParams(vmem_limit_bytes=20 * MIB),
        cost_estimate=pl.CostEstimate(
            flops=4 * frames * width * columns, bytes_accessed=2 * frames * width * 4, transcendentals=frames * columns
        ),
        name="gate",
    )(left_frames, audio, gain, weight)


EDGE = 16


def conv_kernel(before_ref, gated_ref, after_ref, taps_ref, pw_ref, *refs):
    term_ref, padded, act = refs[-3:]
    frames, columns = gated_ref.shape
    taps = taps_ref.shape[0]
    padded[:EDGE] = before_ref[...].astype(jnp.float32)
    padded[EDGE : EDGE + frames] = gated_ref[...].astype(jnp.float32)
    padded[EDGE + frames :] = after_ref[...].astype(jnp.float32)
    chunk = 64
    lead = EDGE - (taps - 1) // 2
    for at in range(0, columns, 128):
        lanes = slice(at, min(at + 128, columns))

        def body(i, carry, lanes=lanes):
            first = pl.multiple_of(i * chunk, chunk)
            window = padded[pl.ds(first, chunk + 2 * EDGE), lanes]
            total = jnp.zeros((chunk, window.shape[1]), jnp.float32)
            for turn in range(8):
                turned_by = window if turn == 0 else pltpu.roll(window, window.shape[0] - turn, 0)
                for offset in range(turn, lead + taps, 8):
                    if offset >= lead:
                        start = offset - turn
                        total = total + turned_by[start : start + chunk] * taps_ref[offset - lead, lanes][None]
            value = total * (1.0 / (1.0 + jnp.exp(-total)))
            act[pl.ds(first, chunk), lanes] = value.astype(jnp.bfloat16)
            return carry

        lax.fori_loop(0, frames // chunk, body, 0)
    pooled = jnp.dot(pooling(frames), act[...], preferred_element_type=jnp.float32).astype(jnp.bfloat16)
    term_ref[...] = jnp.dot(pooled, pw_ref[...], preferred_element_type=jnp.float32).astype(term_ref.dtype)


def conv(before, gated, after, taps, pw, *after_these):
    frames, columns = gated.shape
    vmem = pl.BlockSpec(memory_space=pltpu.VMEM)
    return pl.pallas_call(
        conv_kernel,
        in_specs=[vmem] * 5 + [pl.BlockSpec(memory_space=pl.ANY)] * len(after_these),
        out_specs=vmem,
        out_shape=jax.ShapeDtypeStruct((frames // 4, pw.shape[1]), jnp.bfloat16),
        scratch_shapes=[
            pltpu.VMEM((frames + 2 * EDGE, columns), jnp.float32),
            pltpu.VMEM((frames, columns), jnp.bfloat16),
        ],
        compiler_params=pltpu.CompilerParams(vmem_limit_bytes=12 * MIB),
        cost_estimate=pl.CostEstimate(
            flops=5_000_000_000, bytes_accessed=2 * frames * columns * 4, transcendentals=frames * columns
        ),
        name="conv",
    )(before, gated, after, taps, pw, *after_these)


def place(shift_x, shift_y):
    return [
        ((x * NY + y) * 2 + c, ((x + shift_x) % NX * NY + (y + shift_y) % NY) * 2 + c)
        for x in range(NX)
        for y in range(NY)
        for c in range(2)
    ]


SWAP = [(i, i ^ 1) for i in range(NX * NY * 2)]


def of_group(group, pairs):
    count = NX * NY * 2
    return [(group * count + i, group * count + j) for i, j in pairs]


def spread(block):
    send = lambda v, dx, dy: lax.ppermute(v, ("grp", "seq"), of_group(0, place(dx, dy)))
    rows = block.shape[0]
    near = jnp.concatenate([send(block, 0, 1), block, send(block, 0, -1)], axis=0)
    line = jnp.concatenate([near, send(near, 0, -3), send(near[rows:], 0, 3)], axis=0)
    steps = [-1, 0, 1, 2, 3, 4, -3, -2]
    return [(0, steps, line)] + [(dx, steps, send(line, -dx, 0)) for dx in (-1, 1, 2)]


def tokens_kernel(*refs, counts):
    pieces = refs[: len(counts)]
    audio_ref, term_ref, other_ref, expand_ref = refs[len(counts) : len(counts) + 4]
    out_ref, weight = refs[-2:]
    at = 0
    for ref, count in zip(pieces, counts, strict=True):
        weight[at : at + count] = ref[...]
        at += count
    pooled = (audio_ref[...] + term_ref[...] + other_ref[...].astype(jnp.float32)).astype(jnp.bfloat16)
    ordered = jnp.dot(pooled, expand_ref[...], preferred_element_type=jnp.float32).astype(jnp.bfloat16)
    out_ref[...] = jnp.dot(ordered, weight[...], preferred_element_type=jnp.float32).astype(out_ref.dtype)


def tokens_part(pieces, pooled_audio, term, other, expand, *after_these):
    counts = [p.shape[0] for p in pieces]
    count = pooled_audio.shape[0]
    columns = pieces[0].shape[1]
    vmem = pl.BlockSpec(memory_space=pltpu.VMEM)
    return pl.pallas_call(
        functools.partial(tokens_kernel, counts=counts),
        in_specs=[vmem] * (len(pieces) + 4) + [pl.BlockSpec(memory_space=pl.ANY)] * len(after_these),
        out_specs=vmem,
        out_shape=jax.ShapeDtypeStruct((count, columns), jnp.bfloat16),
        scratch_shapes=[pltpu.VMEM((sum(counts), columns), jnp.bfloat16)],
        compiler_params=pltpu.CompilerParams(vmem_limit_bytes=20 * MIB),
        cost_estimate=pl.CostEstimate(
            flops=4 * count * sum(counts) * columns, bytes_accessed=8000000, transcendentals=0
        ),
        name="tokens_part",
    )(*pieces, pooled_audio, term, other, expand, *after_these)


def shards(
    audio, frame_count, ln_gain, glu_weight, dw_kernel, pw_weight, adapt_weight, text, norm_gain, qkv_weight, qkv_bias
):
    grp = lax.axis_index("grp")
    mdl = lax.axis_index("mdl")
    seq = lax.axis_index("seq")
    core, y, x = seq % 2, seq // 2 % NY, seq // (2 * NY)
    n_mdl = lax.axis_size("mdl")
    both = ("grp", "mdl")
    rows, width = adapt_weight.shape
    ring = lambda group, k: [(group * n_mdl + i, group * n_mdl + (i + k) % n_mdl) for i in range(n_mdl)]

    weight = lax.all_gather(qkv_weight, "seq", axis=0, tiled=True)
    pieces = spread(adapt_weight)
    swap = lambda v: lax.ppermute(v, ("grp", "seq"), of_group(0, SWAP))
    adapter = [p for _, _, p in pieces]
    adapter += [swap(adapter[0]), swap(jnp.concatenate(adapter[1:], axis=0))]

    behind = lax.ppermute(text, both, ring(1, 1))
    ahead = lax.ppermute(text, both, ring(1, -1))
    second = lax.ppermute(behind, both, ring(1, 1))
    words = [text, ahead, second, behind]

    frames = audio.shape[0]
    gated, pooled_audio = gate(
        frame_count - seq * frames, audio, ln_gain[None], jnp.swapaxes(glu_weight, 1, 2)
    )
    up = [(i, i + 1) for i in range(lax.axis_size("seq") - 1)]
    before_edge = lax.ppermute(gated[frames - EDGE :], ("grp", "seq"), of_group(0, up))
    after_edge = lax.ppermute(gated[:EDGE], ("grp", "seq"), of_group(0, [(j, i) for i, j in up]))
    term = conv(before_edge, gated, after_edge, dw_kernel, pw_weight, behind, ahead)
    term = term.astype(jnp.float32) + lax.ppermute(
        term, both, [(0, 1), (1, 0), (2, 3), (3, 2)]
    ).astype(jnp.float32)
    other = lax.ppermute(term.astype(jnp.bfloat16), both, [(1, 2), (2, 1), (3, 0), (0, 3)])

    chips = jnp.concatenate(
        [
            jnp.stack([(x + dx) % NX * NY + (y + dy) % NY for dy in steps])
            for dx, steps, _ in pieces
        ]
    )
    device = jnp.concatenate([2 * chips + core, 2 * chips + 1 - core])
    source = (device[:, None] * rows + jnp.arange(rows, dtype=jnp.int32)[None]).reshape(-1)
    expand = (jnp.arange(audio.shape[1], dtype=jnp.int32)[:, None] == source[None]).astype(jnp.bfloat16)
    tokens = tokens_part(adapter, pooled_audio, term, other, expand, second)

    tables = rotary_tables(2 * text.shape[0])
    gain = norm_gain.reshape(n_mdl, 1, width)
    order = (mdl + jnp.arange(n_mdl, dtype=jnp.int32)) % n_mdl
    same = lax.ppermute(tokens, both, [(i, n_mdl + i) for i in range(n_mdl)])
    following = lax.ppermute(tokens, both, [(i, n_mdl + (i - 1) % n_mdl) for i in range(n_mdl)])
    across = lax.ppermute(following, both, ring(1, -1))
    last = lax.ppermute(same, both, ring(1, 1))
    sounds = [same, following, across, last]
    context = decode(order, words, sounds, gain, weight, qkv_bias[None], tables)
    return jnp.where(grp == 0, tokens, context)[None]


def solution(mesh):
    in_specs = (
        P("seq", None),
        P(),
        P(),
        P(None, None, "mdl"),
        P(None, "mdl"),
        P("mdl", None),
        P("seq", "mdl"),
        P("seq", "mdl"),
        P(),
        P("seq", "mdl"),
        P("mdl"),
    )
    out_specs = P("grp", "seq", "mdl")
    return jax.shard_map(shards, mesh=mesh, in_specs=in_specs, out_specs=out_specs, check_vma=False)
```
